32 devices in a mesh: chan: 4 (over x, core), row: 8 (over z, y).
Axes of the slice: x: 2, y: 2, z: 4, core: 2. Of those that a mesh axis runs over, the one named last changes fastest.
Arguments:
- samples: bfloat16 [8, 128, 65536], P(None, 'chan', 'row'), may hold values from -6 to 6
- history: bfloat16 [8, 128, 7168], P(None, 'chan'), may hold values from -6 to 6
- antenna_flags: int32 [1024], replicated, may hold values 0 or 1
- beam_delays: int32 [256, 1024], replicated, may hold values from 0 to 1023
Outputs:
- visibilities: bfloat16 [512, 2, 1024, 1024], P('chan', None, 'row')
- beam_series: float32 [256, 64, 1024], P(('chan', 'row'))
The draws below stay inside these ranges and needn't reach their ends.
All inputs are finite; a program needn't handle non-finite values.
Results may differ from the reference program's by a relative error of at most 0.0075.
Values may be sent and summed in bfloat16 or wider, within the bound.
No kernel may reach another device: no remote copies, remote signals or barrier semaphores. Data moves between devices by JAX's collectives and lax.ppermute only.
A program may use at most 320 MiB of HBM per device.

```python
import math
import jax
import jax.numpy as jnp
from jax import lax

A = 1024
FOURIER_LENGTH = 1024
NCH = 512
FILTER_TAPS = 8
BEAMS = 256
FR = 8
F = 64
N_ROW = 8


def with_ends(values, stream_key, least, high):
    dims = values.shape
    place = [jax.random.randint(jax.random.fold_in(stream_key, axis), (), 0, dims[axis]) for axis in range(len(dims))]
    values = values.at[tuple(place)].set(least)
    longest = dims.index(max(dims))
    place[longest] = (place[longest] + 1) % dims[longest]
    return values.at[tuple(place)].set(high)


def shard_levels(own_key, dims, split, low, high):
    gain = 1.0
    for dim, blocks in split:
        draws = jax.random.uniform(jax.random.fold_in(jax.random.fold_in(own_key, 6), dim), (blocks,), jnp.float32, low / len(split), high / len(split))
        gain = gain * jnp.repeat(jnp.exp(draws), dims[dim] // blocks).reshape((-1,) + (1,) * (len(dims) - 1 - dim))
    return gain


def gaussian(stream_key, extent, deviation, reach, shards=(), kind=jnp.bfloat16):
    level = shard_levels(stream_key, extent, shards, -0.22, 0.18) if shards else 1.0
    values = jax.random.normal(stream_key, extent, jnp.float32) * deviation * level
    return jnp.minimum(jnp.maximum(values, -reach), reach).astype(kind)


def setup_inputs(seed: int = 0) -> dict:
    keys = jax.random.split(jax.random.key(seed), 5)
    return {
        "samples": gaussian(keys[0], (N_ROW, A // N_ROW, F * FOURIER_LENGTH), 1.0, 6.0, ((1, 4), (2, 8))),
        "history": gaussian(keys[1], (N_ROW, A // N_ROW, (FILTER_TAPS - 1) * FOURIER_LENGTH), 1.0, 6.0, ((1, 4),)),
        "antenna_flags": with_ends((jax.random.randint(keys[2], (A,), 0, 8) < 7).astype(jnp.int32), jax.random.fold_in(keys[2], 1), 0, 1),
        "beam_delays": with_ends(jax.random.randint(keys[3], (BEAMS, A), 0, FOURIER_LENGTH), jax.random.fold_in(keys[3], 1), 0, FOURIER_LENGTH - 1).astype(jnp.int32),
    }


def tap_table():
    position = jnp.arange(FILTER_TAPS * FOURIER_LENGTH, dtype=jnp.int32).astype(jnp.float32) + 0.5
    centred = position / FOURIER_LENGTH - FILTER_TAPS / 2.0
    window = 0.5 - 0.5 * jnp.cos(2.0 * math.pi * position / (FILTER_TAPS * FOURIER_LENGTH))
    return (jnp.sinc(centred) * window).reshape(FILTER_TAPS, FOURIER_LENGTH)

def dft_table():
    sample_ids = jnp.arange(FOURIER_LENGTH, dtype=jnp.int32)
    chan_ids = jnp.arange(NCH, dtype=jnp.int32)
    phase_angle = (sample_ids[:, None] * chan_ids[None, :] % FOURIER_LENGTH).astype(jnp.float32) * (2.0 * math.pi / FOURIER_LENGTH)
    scale = 1.0 / math.sqrt(FOURIER_LENGTH)
    return jnp.stack([jnp.cos(phase_angle) * scale, -jnp.sin(phase_angle) * scale], axis=1).astype(jnp.bfloat16)

def synth_table():
    chan_ids = jnp.arange(NCH, dtype=jnp.int32)
    sample_ids = jnp.arange(FOURIER_LENGTH, dtype=jnp.int32)
    phase_angle = (chan_ids[:, None] * sample_ids[None, :] % FOURIER_LENGTH).astype(jnp.float32) * (2.0 * math.pi / FOURIER_LENGTH)
    scale = 1.0 / math.sqrt(NCH)
    return jnp.stack([jnp.cos(phase_angle) * scale, -jnp.sin(phase_angle) * scale], axis=0).astype(jnp.bfloat16)

def steering(delay_rows, chan_ids):
    delay_index = delay_rows[None, :, :] * chan_ids[:, None, None] % FOURIER_LENGTH
    phase_angle = delay_index.astype(jnp.float32) * (2.0 * math.pi / FOURIER_LENGTH)
    scale = 1.0 / math.sqrt(A)
    return ((jnp.cos(phase_angle) * scale).astype(jnp.bfloat16), (-jnp.sin(phase_angle) * scale).astype(jnp.bfloat16))

def reference(samples, history, antenna_flags, beam_delays):
    frames = FR * N_ROW
    antenna_samples = samples.reshape(A, frames * FOURIER_LENGTH)
    earlier = history.reshape(A, (FILTER_TAPS - 1) * FOURIER_LENGTH)
    extended = jnp.concatenate([earlier, antenna_samples], axis=1).reshape(A, frames + FILTER_TAPS - 1, FOURIER_LENGTH)
    tap_weights = tap_table()
    filter_output = jnp.zeros((A, frames, FOURIER_LENGTH), jnp.float32)
    for tap in range(FILTER_TAPS):
        filter_output = filter_output + extended[:, tap:tap + frames, :].astype(jnp.float32) * tap_weights[tap]
    filter_output = filter_output.astype(jnp.bfloat16)
    spectra = jnp.dot(filter_output.reshape(A * frames, FOURIER_LENGTH).astype(jnp.float32), dft_table().reshape(FOURIER_LENGTH, 2 * NCH).astype(jnp.float32), preferred_element_type=jnp.float32)
    spectra = spectra.astype(jnp.bfloat16).reshape(A, frames, 2, NCH)
    spectra = spectra * antenna_flags.astype(jnp.bfloat16)[:, None, None, None]
    per_chan = spectra.transpose(3, 0, 2, 1).reshape(NCH, A, 2 * frames)
    chan_ids = jnp.arange(NCH, dtype=jnp.int32)

    def per_channel(chan_item):
        values, chan_index = chan_item
        wide = values.astype(jnp.float32)
        swapped = jnp.concatenate([wide[:, frames:], -wide[:, :frames]], axis=1)
        real_part = jnp.dot(wide, wide.T, preferred_element_type=jnp.float32)
        imag_part = jnp.dot(swapped, wide.T, preferred_element_type=jnp.float32)
        products = (jnp.stack([real_part, imag_part]) / frames).astype(jnp.bfloat16)
        w_real, w_imag = steering(beam_delays, chan_index[None])
        w_real = w_real[0].astype(jnp.float32)
        w_imag = w_imag[0].astype(jnp.float32)
        x_real = wide[:, :frames]
        x_imag = wide[:, frames:]
        beam_real = jnp.dot(w_real, x_real, preferred_element_type=jnp.float32) - jnp.dot(w_imag, x_imag, preferred_element_type=jnp.float32)
        beam_imag = jnp.dot(w_real, x_imag, preferred_element_type=jnp.float32) + jnp.dot(w_imag, x_real, preferred_element_type=jnp.float32)
        return (products, jnp.stack([beam_real, beam_imag]))
    visibilities, beam_spectra = lax.map(per_channel, (per_chan, chan_ids))
    beam_spectra = beam_spectra.transpose(2, 1, 0, 3).astype(jnp.bfloat16)
    beam_series = jnp.einsum('bekf,ekn->bfn', beam_spectra.astype(jnp.float32), synth_table().astype(jnp.float32), preferred_element_type=jnp.float32)
    return (visibilities, beam_series)
```

```python
import functools
import math

import jax
import jax.numpy as jnp
from jax import lax
from jax.experimental import pallas as pl
from jax.experimental.pallas import tpu as pltpu
from jax.sharding import PartitionSpec as P

A = 1024
FOURIER_LENGTH = 1024
NCH = 512
FILTER_TAPS = 8
BEAMS = 256
LANES = 128
CHUNKS = 8
VMEM = pl.BlockSpec(memory_space=pltpu.VMEM)
ANY = pl.BlockSpec(memory_space=pl.ANY)


def params(mib):
    return pltpu.CompilerParams(vmem_limit_bytes=mib * 2**20)


def cost(flops, bytes_accessed):
    return pl.CostEstimate(flops=int(flops), bytes_accessed=int(bytes_accessed), transcendentals=0)


def from_behind(block, axis, distance):
    devices = range(lax.axis_size(axis))
    route = [(i - distance, i) for i in devices if i - distance in devices]
    return lax.ppermute(block, axis, route)


def tap_table():
    position = jnp.arange(FILTER_TAPS * FOURIER_LENGTH, dtype=jnp.int32).astype(jnp.float32) + 0.5
    centred = position / FOURIER_LENGTH - FILTER_TAPS / 2.0
    window = 0.5 - 0.5 * jnp.cos(2.0 * math.pi * position / (FILTER_TAPS * FOURIER_LENGTH))
    return (jnp.sinc(centred) * window).reshape(FILTER_TAPS, FOURIER_LENGTH)


def dft_rows(channel_number):
    chan_ids = jnp.arange(NCH, dtype=jnp.int32).reshape(channel_number, 1, -1, 1)
    sample_ids = jnp.arange(FOURIER_LENGTH, dtype=jnp.int32)
    phase_angle = (chan_ids * sample_ids % FOURIER_LENGTH).astype(jnp.float32) * (
        2.0 * math.pi / FOURIER_LENGTH
    )
    scale = 1.0 / math.sqrt(FOURIER_LENGTH)
    table = jnp.concatenate([jnp.cos(phase_angle) * scale, -jnp.sin(phase_angle) * scale], axis=1)
    return table.astype(jnp.bfloat16).reshape(channel_number, -1, FOURIER_LENGTH)


def synth_table():
    chan_ids = jnp.arange(NCH, dtype=jnp.int32)
    sample_ids = jnp.arange(FOURIER_LENGTH, dtype=jnp.int32)
    phase_angle = (chan_ids[:, None] * sample_ids[None, :] % FOURIER_LENGTH).astype(jnp.float32) * (
        2.0 * math.pi / FOURIER_LENGTH
    )
    scale = 1.0 / math.sqrt(NCH)
    return jnp.stack([jnp.cos(phase_angle) * scale, -jnp.sin(phase_angle) * scale], axis=0).astype(
        jnp.bfloat16
    )


def phasor(delays, chan_ids, scale):
    angle = (delays * chan_ids % FOURIER_LENGTH).astype(jnp.float32) * (
        2.0 * math.pi / FOURIER_LENGTH
    )
    return jnp.cos(angle) * scale, -jnp.sin(angle) * scale


def front_kernel(rows, steps, parcels, place, samples, before, history, taps, table, *refs):
    outs, (filtered, wide) = refs[:-2], refs[-2:]
    step = pl.program_id(0)
    frames = samples.shape[1] // FOURIER_LENGTH
    past = FILTER_TAPS - 1
    group = min(16, rows)

    @pl.when(step < steps)
    def _():
        first = place[1] == 0

        def columns(i, carry):
            at = pl.multiple_of(i * LANES, LANES)
            weights = [
                jnp.broadcast_to(taps[t : t + 1, pl.ds(at, LANES)], (group, LANES))
                for t in range(FILTER_TAPS)
            ]
            for g in range(rows // group):
                here = slice(g * group, (g + 1) * group)
                values = []
                for frame in range(past):
                    lanes = pl.ds(at + frame * FOURIER_LENGTH, LANES)
                    values.append(
                        jnp.where(
                            first,
                            history[here, lanes].astype(jnp.float32),
                            before[here, lanes].astype(jnp.float32),
                        )
                    )
                for frame in range(frames):
                    lanes = pl.ds(at + frame * FOURIER_LENGTH, LANES)
                    values.append(samples[here, lanes].astype(jnp.float32))
                for frame in range(frames):
                    total = values[frame] * weights[0]
                    for t in range(1, FILTER_TAPS):
                        total = total + values[frame + t] * weights[t]
                    filtered[
                        frame, pl.ds(step * rows + g * group, group), pl.ds(at, LANES)
                    ] = total.astype(jnp.bfloat16)
            return carry

        lax.fori_loop(0, FOURIER_LENGTH // LANES, columns, 0)

    count = table.shape[0] // 2
    antennas = filtered.shape[1]
    width = wide.shape[2]
    parts = antennas // width
    for m in range(len(outs) // len(parcels)):

        @pl.when(step == steps + m)
        def _(m=m):
            for frame in range(frames):
                got = lax.dot_general(
                    table[...],
                    filtered[frame],
                    (((1,), (1,)), ((), ())),
                    preferred_element_type=jnp.float32,
                )
                for part in range(parts):
                    lanes = slice(part * width, (part + 1) * width)
                    wide[part, pl.ds(frame, count, stride=2 * frames), :] = got[:count, lanes]
                    wide[part, pl.ds(frames + frame, count, stride=2 * frames), :] = got[
                        count:, lanes
                    ]
            start = 0
            for p, size in enumerate(parcels):
                out = outs[m * len(parcels) + p]
                for part in range(parts):
                    lanes = slice(part * width, (part + 1) * width)
                    out[:, lanes] = wide[
                        part, start * 2 * frames : (start + size) * 2 * frames, :
                    ].astype(jnp.bfloat16)
                start += size


def front(samples, before, history, place, channel_number, parcels):
    antennas, length = samples.shape
    frames = length // FOURIER_LENGTH
    channel_total = NCH // channel_number
    rows = min(32, antennas)
    steps = antennas // rows
    width = min(LANES, antennas)
    past = (FILTER_TAPS - 1) * FOURIER_LENGTH
    grid_spec = pltpu.PrefetchScalarGridSpec(
        num_scalar_prefetch=1,
        grid=(steps + channel_number,),
        in_specs=[
            pl.BlockSpec((rows, length), lambda i, s: (jnp.minimum(i, steps - 1), 0)),
            pl.BlockSpec((rows, past), lambda i, s: (jnp.minimum(i, steps - 1), 0)),
            pl.BlockSpec((rows, past), lambda i, s: (jnp.minimum(i, steps - 1), 0)),
            VMEM,
            pl.BlockSpec(
                (None, 2 * channel_total, FOURIER_LENGTH),
                lambda i, s: (lax.rem(s[0] + jnp.maximum(i - steps, 0), channel_number), 0, 0),
            ),
        ],
        out_specs=[VMEM] * (channel_number * len(parcels)),
        scratch_shapes=[
            pltpu.VMEM((frames, antennas, FOURIER_LENGTH), jnp.bfloat16),
            pltpu.VMEM((antennas // width, channel_total * 2 * frames, width), jnp.float32),
        ],
    )
    return pl.pallas_call(
        functools.partial(front_kernel, rows, steps, parcels),
        grid_spec=grid_spec,
        out_shape=[
            jax.ShapeDtypeStruct((size * 2 * frames, antennas), jnp.bfloat16)
            for _ in range(channel_number)
            for size in parcels
        ],
        compiler_params=params(48),
        cost_estimate=cost(2 * antennas * frames * FOURIER_LENGTH * 2 * NCH * 2, 16 * 2**20),
        name="front",
    )(place, samples, before, history, tap_table(), dft_rows(channel_number))


def order_kernel(number, *refs):
    pieces, spread, outs = refs[:number], refs[number], refs[number + 1 :]
    rows = outs[0].shape[0]
    tile = math.gcd(rows, 256)
    for j, out in enumerate(outs):

        def part(i, carry, out=out, j=j):
            at = pl.multiple_of(i * tile, tile)
            total = None
            for m, piece in enumerate(pieces):
                got = jnp.dot(
                    piece[pl.ds(j * rows + at, tile), :],
                    spread[m],
                    preferred_element_type=jnp.float32,
                )
                total = got if total is None else total + got
            out[pl.ds(at, tile), :] = total.astype(jnp.bfloat16)
            return carry

        lax.fori_loop(0, rows // tile, part, 0)


def into_order(pieces, spread, chunks, rows):
    return pl.pallas_call(
        functools.partial(order_kernel, len(pieces)),
        in_specs=[VMEM] * (len(pieces) + 1),
        out_specs=[VMEM] * chunks,
        out_shape=[jax.ShapeDtypeStruct((rows, A), jnp.bfloat16)] * chunks,
        compiler_params=params(40),
        cost_estimate=cost(2 * chunks * rows * A * A * 2, chunks * rows * A * 4),
        name="into_order",
    )(*pieces, spread)


def spread_table(antenna_flags, chan_id, channel_number, block_list):
    per_shard = A // (channel_number * block_list)
    block = (chan_id - jnp.arange(channel_number, dtype=jnp.int32)) % channel_number
    own = jnp.arange(block_list * per_shard, dtype=jnp.int32)
    target = (
        (own // per_shard) * (A // block_list) + block[:, None] * per_shard + own % per_shard
    )
    hit = target[:, :, None] == jnp.arange(A, dtype=jnp.int32)
    return jnp.where(hit, antenna_flags, 0).astype(jnp.bfloat16)


def visibility_kernel(number, frames, aliased, place, *refs):
    pieces, out = refs[:number], refs[-1]
    half = pieces[0].shape[1] // 2
    row_count = out.shape[2]
    own_lanes = pl.ds(pl.multiple_of(place[1] * row_count, row_count), row_count)
    for i in range(pieces[0].shape[0]):
        everything = jnp.concatenate([piece[i] for piece in pieces], axis=0)
        own = jnp.concatenate([piece[i, :, own_lanes] for piece in pieces], axis=0)
        wide = own.astype(jnp.float32)
        swapped = jnp.concatenate(
            [
                part
                for s in range(number)
                for part in (
                    wide[(2 * s + 1) * half : (2 * s + 2) * half],
                    -wide[2 * s * half : (2 * s + 1) * half],
                )
            ],
            axis=0,
        )
        for e, left in enumerate((wide, swapped)):
            got = jnp.dot(
                left.T.astype(jnp.bfloat16), everything, preferred_element_type=jnp.float32
            )
            out[i, e] = (got * (1.0 / frames)).astype(jnp.bfloat16)


def visibilities_of(pieces, place, target, first, channel_total, row_count, frames):
    count = pieces[0].shape[0]
    block = math.gcd(count, 4)
    offset = first // block
    aliased = target is not None
    in_specs = [
        pl.BlockSpec((block,) + pieces[0].shape[1:], lambda i, s: (i, 0, 0)) for _ in pieces
    ]
    return pl.pallas_call(
        functools.partial(visibility_kernel, len(pieces), frames, aliased),
        grid_spec=pltpu.PrefetchScalarGridSpec(
            num_scalar_prefetch=1,
            grid=(count // block,),
            in_specs=in_specs + [ANY] * aliased,
            out_specs=pl.BlockSpec(
                (block, 2, row_count, A), lambda i, s: (i + offset, 0, 0, 0)
            ),
        ),
        out_shape=jax.ShapeDtypeStruct((channel_total, 2, row_count, A), jnp.bfloat16),
        input_output_aliases={1 + len(pieces): 0} if aliased else {},
        compiler_params=params(40),
        cost_estimate=cost(8 * count * row_count * A * 256, count * row_count * A * 4),
        name="visibilities",
    )(place, *pieces, *([target] if aliased else []))


def beam_kernel(number, *refs):
    pieces = refs[:number]
    base_re, base_im, step_re, step_im, out, state_re, state_im = refs[number:]
    half = pieces[0].shape[1] // 2
    beams = base_re.shape[0]

    @pl.when(pl.program_id(0) == 0)
    def _():
        state_re[...] = base_re[...]
        state_im[...] = base_im[...]

    for i in range(pieces[0].shape[0]):
        now_re, now_im = state_re[...], state_im[...]
        weights = jnp.concatenate([now_re, now_im], axis=0).astype(jnp.bfloat16)
        state_re[...] = now_re * step_re[...] - now_im * step_im[...]
        state_im[...] = now_re * step_im[...] + now_im * step_re[...]
        everything = jnp.concatenate([piece[i] for piece in pieces], axis=0)
        got = lax.dot_general(
            weights, everything, (((1,), (1,)), ((), ())), preferred_element_type=jnp.float32
        )
        direct, crossed = got[:beams], got[beams:]
        width = got.shape[1]
        lane = lax.broadcasted_iota(jnp.int32, crossed.shape, 1)
        real_lane = lax.rem(lane, 2 * half) < half
        crossed = jnp.where(
            real_lane,
            -pltpu.roll(crossed, width - half, 1),
            pltpu.roll(crossed, half, 1),
        )
        out[i] = (direct + crossed).astype(jnp.bfloat16)


def beams_of(pieces, base_re, base_im, step_re, step_im):
    count, rows, _ = pieces[0].shape
    number = len(pieces)
    beams = step_re.shape[0]
    block = math.gcd(count, 4)
    whole = pl.BlockSpec((beams, A), lambda i: (0, 0))
    return pl.pallas_call(
        functools.partial(beam_kernel, number),
        grid=(count // block,),
        in_specs=[pl.BlockSpec((block, rows, A), lambda i: (i, 0, 0)) for _ in pieces]
        + [whole] * 4,
        out_specs=pl.BlockSpec((block, beams, number * rows), lambda i: (i, 0, 0)),
        out_shape=jax.ShapeDtypeStruct((count, beams, number * rows), jnp.bfloat16),
        scratch_shapes=[pltpu.VMEM((beams, A), jnp.float32)] * 2,
        compiler_params=params(40),
        cost_estimate=cost(8 * count * beams * A * 256, count * number * rows * A * 2),
        name="beams",
    )(*pieces, base_re, base_im, step_re, step_im)


def synthesis_kernel(number, half, owners, spectra, table, out):
    got = [
        lax.dot_general(
            spectra[...], table[e], (((0,), (0,)), ((), ())), preferred_element_type=jnp.float32
        )
        for e in range(2)
    ]
    for s in range(number):
        real, imag = 2 * s * half, (2 * s + 1) * half
        at = pl.multiple_of(owners[s] * half, half)
        out[pl.ds(at, half), :] = got[0][real : real + half] + got[1][imag : imag + half]


def synthesis(spectra, owners, frames):
    beam_count, channels, width = spectra.shape
    number = owners.shape[0]
    return pl.pallas_call(
        functools.partial(synthesis_kernel, number, frames // number),
        grid_spec=pltpu.PrefetchScalarGridSpec(
            num_scalar_prefetch=1,
            grid=(beam_count,),
            in_specs=[pl.BlockSpec((None, channels, width), lambda i, s: (i, 0, 0)), VMEM],
            out_specs=pl.BlockSpec((None, frames, FOURIER_LENGTH), lambda i, s: (i, 0, 0)),
        ),
        out_shape=jax.ShapeDtypeStruct((beam_count, frames, FOURIER_LENGTH), jnp.float32),
        compiler_params=params(40),
        cost_estimate=cost(4 * beam_count * channels * width * FOURIER_LENGTH, 8 * 2**20),
        name="synthesis",
    )(owners, spectra, synth_table())


def body(samples, history, antenna_flags, beam_delays):
    channel_number = lax.axis_size("chan")
    n_row = lax.axis_size("row")
    chan_id = lax.axis_index("chan")
    row_id = lax.axis_index("row")
    block_list, antennas_per_shard, shard_length = samples.shape
    frames_per_shard = shard_length // FOURIER_LENGTH
    frames = frames_per_shard * n_row
    channel_total = NCH // channel_number
    row_count = A // n_row
    beam_count = BEAMS // (channel_number * n_row)
    antennas = block_list * antennas_per_shard
    chunk = channel_total // CHUNKS
    chunk_rows = chunk * 2 * frames_per_shard
    place = jnp.stack([chan_id, row_id]).astype(jnp.int32)

    cycle = [i for i in range(n_row) if i % 2 == 0] + [i for i in reversed(range(n_row)) if i % 2]
    onward = [(cycle[i], cycle[(i + 1) % n_row]) for i in range(n_row)]
    backward = [(b, a) for a, b in onward]
    position = jnp.array([cycle.index(i) for i in range(n_row)], jnp.int32)[row_id]
    owners = jnp.array(cycle, jnp.int32)[
        (position - jnp.arange(n_row, dtype=jnp.int32)) % n_row
    ]

    tail = samples[:, :, shard_length - (FILTER_TAPS - 1) * FOURIER_LENGTH :]
    before = from_behind(tail, "row", 1)

    parcels = [2, CHUNKS - 2]
    sent = front(
        samples.reshape(antennas, -1),
        before.reshape(antennas, -1),
        history.reshape(antennas, -1),
        place,
        channel_number,
        [p * chunk for p in parcels],
    )
    spread = spread_table(antenna_flags, chan_id, channel_number, block_list)
    chunks = []
    for p, size in enumerate(parcels):
        pieces = []
        for m in range(channel_number):
            piece = sent[m * len(parcels) + p]
            if m:
                route = [(i, (i + m) % channel_number) for i in range(channel_number)]
                piece = lax.ppermute(piece, "chan", route)
            pieces.append(piece)
        chunks += into_order(pieces, spread, size, chunk_rows)

    delays = lax.dynamic_index_in_dim(
        beam_delays.reshape(channel_number, n_row, beam_count, A), row_id, 1, keepdims=False
    ).reshape(channel_number * beam_count, A)
    starts = chan_id * channel_total + chunk * jnp.arange(CHUNKS, dtype=jnp.int32)
    base_re, base_im = phasor(delays[None], starts[:, None, None], 1.0 / math.sqrt(A))
    step_re, step_im = phasor(delays, 1, 1.0)

    visibilities = None
    beams = []
    for j in range(CHUNKS):
        piece = chunks[j].reshape(chunk, 2 * frames_per_shard, A)
        held = [piece]
        for _ in range(n_row - 1):
            piece = lax.ppermute(piece, "row", backward if j % 2 else onward)
            held.append(piece)
        if j % 2:
            held = held[:1] + held[:0:-1]
        beams.append(beams_of(held, base_re[j], base_im[j], step_re, step_im))
        visibilities = visibilities_of(
            held, place, visibilities, j * chunk, channel_total, row_count, frames
        )

    def to_owners(parts):
        value = jnp.concatenate(parts, axis=0)
        value = value.reshape(-1, channel_number, beam_count, 2 * frames).transpose(1, 2, 0, 3)
        return lax.all_to_all(value, "chan", split_axis=0, concat_axis=0, tiled=True)

    arrived = [to_owners(beams[: CHUNKS - 2]), to_owners(beams[CHUNKS - 2 :])]
    spectra = jnp.concatenate(arrived, axis=2).transpose(1, 0, 2, 3)
    beam_series = synthesis(
        spectra.reshape(beam_count, NCH, 2 * frames), owners, frames
    )
    return (visibilities, beam_series)


def solution(mesh):
    in_specs = (P(None, "chan", "row"), P(None, "chan", None), P(), P())
    out_specs = (P("chan", None, "row", None), P(("chan", "row"), None, None))
    return jax.shard_map(body, mesh=mesh, in_specs=in_specs, out_specs=out_specs, check_vma=False)
```

```python
import functools
import math

import jax
import jax.numpy as jnp
from jax import lax
from jax.experimental import pallas as pl
from jax.experimental.pallas import tpu as pltpu
from jax.sharding import PartitionSpec as P

A = 1024
FOURIER_LENGTH = 1024
NCH = 512
FILTER_TAPS = 8
BEAMS = 256
LANES = 128
UNITS = 32
CHUNKS = (4, 6, 6, 6, 4, 2, 2, 2)
LONG = 6
BLOCK = 4
HALVES = 2
VMEM = pl.BlockSpec(memory_space=pltpu.VMEM)
HBM = pl.BlockSpec(memory_space=pltpu.HBM)


def params(mib):
    return pltpu.CompilerParams(vmem_limit_bytes=mib * 2**20)


def cost(flops, bytes_accessed):
    return pl.CostEstimate(flops=int(3 * flops), bytes_accessed=int(3 * bytes_accessed), transcendentals=0)


def from_behind(block, axis, distance):
    devices = range(lax.axis_size(axis))
    route = [(i - distance, i) for i in devices if i - distance in devices]
    return lax.ppermute(block, axis, route)


def tap_table():
    position = jnp.arange(FILTER_TAPS * FOURIER_LENGTH, dtype=jnp.int32).astype(jnp.float32) + 0.5
    centred = position / FOURIER_LENGTH - FILTER_TAPS / 2.0
    window = 0.5 - 0.5 * jnp.cos(2.0 * math.pi * position / (FILTER_TAPS * FOURIER_LENGTH))
    return (jnp.sinc(centred) * window).reshape(FILTER_TAPS, FOURIER_LENGTH)


def dft_rows(channel_number):
    chan_ids = jnp.arange(NCH, dtype=jnp.int32).reshape(channel_number, 1, -1, 1)
    sample_ids = jnp.arange(FOURIER_LENGTH, dtype=jnp.int32)
    phase_angle = (chan_ids * sample_ids % FOURIER_LENGTH).astype(jnp.float32) * (
        2.0 * math.pi / FOURIER_LENGTH
    )
    scale = 1.0 / math.sqrt(FOURIER_LENGTH)
    table = jnp.concatenate([jnp.cos(phase_angle) * scale, -jnp.sin(phase_angle) * scale], axis=1)
    return table.astype(jnp.bfloat16).reshape(channel_number, -1, FOURIER_LENGTH)


def synth_table():
    chan_ids = jnp.arange(NCH, dtype=jnp.int32)
    sample_ids = jnp.arange(FOURIER_LENGTH, dtype=jnp.int32)
    phase_angle = (chan_ids[:, None] * sample_ids[None, :] % FOURIER_LENGTH).astype(jnp.float32) * (
        2.0 * math.pi / FOURIER_LENGTH
    )
    scale = 1.0 / math.sqrt(NCH)
    return jnp.stack([jnp.cos(phase_angle) * scale, -jnp.sin(phase_angle) * scale], axis=0).astype(
        jnp.bfloat16
    )


def phasor(delays, chan_ids, scale):
    angle = (delays * chan_ids % FOURIER_LENGTH).astype(jnp.float32) * (
        2.0 * math.pi / FOURIER_LENGTH
    )
    return jnp.cos(angle) * scale, -jnp.sin(angle) * scale


def front_kernel(rows, steps, fold, parcels, place, samples, before, history, taps, table, *refs):
    outs, (filtered, wide) = refs[:-2], refs[-2:]
    step = pl.program_id(0)
    frames = samples.shape[1] // FOURIER_LENGTH
    past = FILTER_TAPS - 1
    group = min(16, rows)
    antennas = filtered.shape[1] // fold

    @pl.when(step < steps)
    def _():
        first = place[1] == 0

        def columns(i, carry):
            at = pl.multiple_of(i * LANES, LANES)
            weights = [
                jnp.broadcast_to(taps[t : t + 1, pl.ds(at, LANES)], (group, LANES))
                for t in range(FILTER_TAPS)
            ]
            for g in range(rows // group):
                here = slice(g * group, (g + 1) * group)
                values = []
                for frame in range(past):
                    lanes = pl.ds(at + frame * FOURIER_LENGTH, LANES)
                    values.append(
                        jnp.where(
                            first,
                            history[here, lanes].astype(jnp.float32),
                            before[here, lanes].astype(jnp.float32),
                        )
                    )
                for frame in range(frames):
                    lanes = pl.ds(at + frame * FOURIER_LENGTH, LANES)
                    values.append(samples[here, lanes].astype(jnp.float32))
                for frame in range(frames):
                    total = values[frame] * weights[0]
                    for t in range(1, FILTER_TAPS):
                        total = total + values[frame + t] * weights[t]
                    to = (frame % fold) * antennas + g * group
                    filtered[frame // fold, pl.ds(step * rows + to, group), pl.ds(at, LANES)] = (
                        total.astype(jnp.bfloat16)
                    )
            return carry

        lax.fori_loop(0, FOURIER_LENGTH // LANES, columns, 0)

    count = table.shape[0] // 2
    for m in range(len(outs) // len(parcels)):

        @pl.when(step == steps + m)
        def _(m=m):
            for several in range(frames // fold):
                got = lax.dot_general(
                    table[...],
                    filtered[several],
                    (((1,), (1,)), ((), ())),
                    preferred_element_type=jnp.float32,
                )
                for part in range(fold):
                    frame = several * fold + part
                    lanes = slice(part * antennas, (part + 1) * antennas)
                    wide[pl.ds(frame, count, stride=2 * frames), :] = got[:count, lanes]
                    wide[pl.ds(frames + frame, count, stride=2 * frames), :] = got[count:, lanes]
            start = 0
            for p, size in enumerate(parcels):
                outs[m * len(parcels) + p][...] = wide[
                    start * 2 * frames : (start + size) * 2 * frames, :
                ].astype(jnp.bfloat16)
                start += size


def front(samples, before, history, place, taps, table, half, parcels):
    antennas = before.shape[0]
    length = samples.shape[1]
    frames = length // FOURIER_LENGTH
    channel_number, channel_total = table.shape[0], table.shape[1] // 2
    rows = min(32, antennas)
    steps = antennas // rows
    fold = math.gcd(frames, max(1, 256 // antennas))
    past = (FILTER_TAPS - 1) * FOURIER_LENGTH
    grid_spec = pltpu.PrefetchScalarGridSpec(
        num_scalar_prefetch=1,
        grid=(steps + channel_number,),
        in_specs=[
            pl.BlockSpec(
                (rows, length), lambda i, s: (half * steps + jnp.minimum(i, steps - 1), 0)
            ),
            pl.BlockSpec((rows, past), lambda i, s: (jnp.minimum(i, steps - 1), 0)),
            pl.BlockSpec(
                (rows, past), lambda i, s: (half * steps + jnp.minimum(i, steps - 1), 0)
            ),
            VMEM,
            pl.BlockSpec(
                (None, 2 * channel_total, FOURIER_LENGTH),
                lambda i, s: (lax.rem(s[0] + jnp.maximum(i - steps, 0), channel_number), 0, 0),
            ),
        ],
        out_specs=[VMEM] * (channel_number * len(parcels)),
        scratch_shapes=[
            pltpu.VMEM((frames // fold, fold * antennas, FOURIER_LENGTH), jnp.bfloat16),
            pltpu.VMEM((channel_total * 2 * frames, antennas), jnp.float32),
        ],
    )
    return pl.pallas_call(
        functools.partial(front_kernel, rows, steps, fold, parcels),
        grid_spec=grid_spec,
        out_shape=[
            jax.ShapeDtypeStruct((size * 2 * frames, antennas), jnp.bfloat16)
            for _ in range(channel_number)
            for size in parcels
        ],
        compiler_params=params(16),
        cost_estimate=cost(2 * antennas * frames * FOURIER_LENGTH * 2 * NCH * 2, 8 * 2**20),
        name="front",
    )(place, samples, before, history, taps, table)


def order_kernel(number, halves, *refs):
    pieces, spread, out = refs[:-2], refs[-2], refs[-1]
    total = None
    for m in range(number):
        left = jnp.concatenate(
            [piece[...] for piece in pieces[m * halves : (m + 1) * halves]], axis=1
        )
        got = jnp.dot(left, spread[m], preferred_element_type=jnp.float32)
        total = got if total is None else total + got
    out[...] = total.astype(jnp.bfloat16)


def into_order(pieces, halves, spread, block, blocks):
    number = len(pieces) // halves
    rows = block * blocks
    width = spread.shape[2]
    return pl.pallas_call(
        functools.partial(order_kernel, number, halves),
        grid=(blocks,),
        in_specs=[
            pl.BlockSpec((block, p.shape[1]), lambda i, at=at: (at // block + i, 0))
            for p, at in pieces
        ]
        + [VMEM],
        out_specs=pl.BlockSpec((block, width), lambda i: (i, 0)),
        out_shape=jax.ShapeDtypeStruct((rows, width), jnp.bfloat16),
        compiler_params=params(10),
        cost_estimate=cost(2 * rows * width * width, rows * width * 4),
        name="into_order",
    )(*[p for p, _ in pieces], spread)


def spread_table(antenna_flags, chan_id, channel_number, block_list):
    per_shard = A // (channel_number * block_list)
    block = (chan_id - jnp.arange(channel_number, dtype=jnp.int32)) % channel_number
    own = jnp.arange(block_list * per_shard, dtype=jnp.int32)
    target = (
        (own // per_shard) * (A // block_list) + block[:, None] * per_shard + own % per_shard
    )
    hit = target[:, :, None] == jnp.arange(A, dtype=jnp.int32)
    return jnp.where(hit, antenna_flags, 0).astype(jnp.bfloat16)


def products_kernel(ends, frames, aliased, seen, formed, place, *refs):
    number = len(ends)
    count = sum(map(len, ends))
    pieces = iter(refs[:count])
    sources = [[next(pieces) for _ in slot] for slot in ends]
    base_re, base_im, step_re, step_im = refs[count : count + 4] if formed else [None] * 4
    outs = refs[count + 4 * formed + aliased :]
    out = outs[0] if seen else None
    beam_out, state_re, state_im = outs[seen:] if formed else [None] * 3
    block, rows = sources[0][0].shape[:2]
    half = rows // 2
    step = pl.program_id(0)

    if formed:

        @pl.when(step == 0)
        def _():
            state_re[...] = base_re[...]
            state_im[...] = base_im[...]

    def slots(i, lanes):
        found = []
        for slot, end in zip(sources, ends):
            value = slot[-1][i, :, lanes]
            for source, last in zip(slot[-2::-1], end[-2::-1]):
                value = jnp.where(step < last, source[i, :, lanes], value)
            found.append(value)
        return jnp.concatenate(found, axis=0)

    def visibilities(i, everything):
        row_count = out.shape[2]
        own_lanes = pl.ds(pl.multiple_of(place[1] * row_count, row_count), row_count)
        wide = slots(i, own_lanes).astype(jnp.float32)
        swapped = jnp.concatenate(
            [
                part
                for s in range(number)
                for part in (
                    wide[(2 * s + 1) * half : (2 * s + 2) * half],
                    -wide[2 * s * half : (2 * s + 1) * half],
                )
            ],
            axis=0,
        )
        left = jnp.concatenate([wide.T, swapped.T], axis=0).astype(jnp.bfloat16)
        got = jnp.dot(left, everything, preferred_element_type=jnp.float32)
        got = (got * (1.0 / frames)).astype(jnp.bfloat16)
        out[i, 0] = got[:row_count]
        out[i, 1] = got[row_count:]

    def beams(i, everything):
        now_re, now_im = state_re[...], state_im[...]
        weights = jnp.concatenate([now_re, now_im], axis=0).astype(jnp.bfloat16)
        state_re[...] = now_re * step_re[...] - now_im * step_im[...]
        state_im[...] = now_re * step_im[...] + now_im * step_re[...]
        got = lax.dot_general(
            weights, everything, (((1,), (1,)), ((), ())), preferred_element_type=jnp.float32
        )
        direct, crossed = jnp.split(got, 2, axis=0)
        width = got.shape[1]
        lane = lax.broadcasted_iota(jnp.int32, crossed.shape, 1)
        real_lane = lax.rem(lane, 2 * half) < half
        crossed = jnp.where(
            real_lane,
            -pltpu.roll(crossed, width - half, 1),
            pltpu.roll(crossed, half, 1),
        )
        beam_out[i] = (direct + crossed).astype(jnp.bfloat16)

    for i in range(block):
        everything = slots(i, slice(None))
        if seen:
            visibilities(i, everything)
        if formed:
            beams(i, everything)


def products_of(
    pieces, place, target, weights, first, count, channel_total, row_count, frames, seen, formed
):
    number = len(pieces)
    rows = pieces[0][0][0].shape[1]
    beams = weights[0].shape[0]
    block = math.gcd(first, BLOCK, *[n for slot in pieces for _, _, n in slot])
    ends = [[sum(n for _, _, n in slot[: c + 1]) // block for c in range(len(slot))] for slot in pieces]
    in_specs = []
    for slot, end in zip(pieces, ends):
        for (_, at, n), last in zip(slot, end):
            begin = last - n // block
            in_specs.append(
                pl.BlockSpec(
                    (block, rows, A),
                    lambda i, s, at=at // block, begin=begin, last=last: (
                        at + jnp.clip(i, begin, last - 1) - begin,
                        0,
                        0,
                    ),
                )
            )
    pieces = [p for slot in pieces for p, _, _ in slot]
    offset = first // block
    aliased = seen and target is not None
    out_specs, out_shape = [], []
    if seen:
        out_specs.append(
            pl.BlockSpec((block, 2, row_count, A), lambda i, s: (i + offset, 0, 0, 0))
        )
        out_shape.append(
            jax.ShapeDtypeStruct((channel_total, 2, row_count, A), jnp.bfloat16)
        )
    if formed:
        out_specs.append(pl.BlockSpec((block, beams, number * rows), lambda i, s: (i, 0, 0)))
        out_shape.append(jax.ShapeDtypeStruct((count, beams, number * rows), jnp.bfloat16))
    others = [*weights] * formed + [target] * aliased
    return pl.pallas_call(
        functools.partial(products_kernel, ends, frames, aliased, seen, formed),
        grid_spec=pltpu.PrefetchScalarGridSpec(
            num_scalar_prefetch=1,
            grid=(count // block,),
            in_specs=in_specs
            + [pl.BlockSpec((beams, A), lambda i, s: (0, 0))] * (4 * formed)
            + [HBM] * aliased,
            out_specs=out_specs,
            scratch_shapes=[pltpu.VMEM((beams, A), jnp.float32)] * (2 * formed),
        ),
        out_shape=out_shape,
        input_output_aliases={1 + len(pieces) + 4 * formed: 0} if aliased else {},
        compiler_params=params(10),
        cost_estimate=cost(12 * count * row_count * A * 256, count * row_count * A * 6),
        name="products",
    )(place, *pieces, *others)


def synthesis_kernel(number, half, owners, spectra, table, out):
    got = [
        lax.dot_general(
            spectra[...], table[e], (((0,), (0,)), ((), ())), preferred_element_type=jnp.float32
        )
        for e in range(2)
    ]
    for s in range(number):
        real, imag = 2 * s * half, (2 * s + 1) * half
        rows = pl.ds(pl.multiple_of(owners[s] * half, half), half)
        out[rows, :] = got[0][real : real + half] + got[1][imag : imag + half]


def synthesis(spectra, table, owners, frames):
    beam_count, channels, width = spectra.shape
    number = owners.shape[0]
    return pl.pallas_call(
        functools.partial(synthesis_kernel, number, frames // number),
        grid_spec=pltpu.PrefetchScalarGridSpec(
            num_scalar_prefetch=1,
            grid=(beam_count,),
            in_specs=[pl.BlockSpec((None, channels, width), lambda i, s: (i, 0, 0)), VMEM],
            out_specs=pl.BlockSpec((None, frames, FOURIER_LENGTH), lambda i, s: (i, 0, 0)),
        ),
        out_shape=jax.ShapeDtypeStruct((beam_count, frames, FOURIER_LENGTH), jnp.float32),
        compiler_params=params(10),
        cost_estimate=cost(4 * beam_count * channels * width * FOURIER_LENGTH, 8 * 2**20),
        name="synthesis",
    )(owners, spectra, table)


def body(samples, history, antenna_flags, beam_delays):
    channel_number = lax.axis_size("chan")
    n_row = lax.axis_size("row")
    chan_id = lax.axis_index("chan")
    row_id = lax.axis_index("row")
    block_list, antennas_per_shard, shard_length = samples.shape
    frames_per_shard = shard_length // FOURIER_LENGTH
    frames = frames_per_shard * n_row
    channel_total = NCH // channel_number
    row_count = A // n_row
    beam_count = BEAMS // (channel_number * n_row)
    antennas = block_list * antennas_per_shard
    unit = channel_total // UNITS
    rows_of = 2 * frames_per_shard
    place = jnp.stack([chan_id, row_id]).astype(jnp.int32)

    cycle = [i for i in range(n_row) if i % 2 == 0] + [i for i in reversed(range(n_row)) if i % 2]
    onward = [(cycle[i], cycle[(i + 1) % n_row]) for i in range(n_row)]
    backward = [(b, a) for a, b in onward]
    position = jnp.array([cycle.index(i) for i in range(n_row)], jnp.int32)[row_id]
    owners = jnp.array(cycle, jnp.int32)[
        (position - jnp.arange(n_row, dtype=jnp.int32)) % n_row
    ]

    past = (FILTER_TAPS - 1) * FOURIER_LENGTH
    blocks = block_list // HALVES
    before = [
        from_behind(samples[h * blocks : (h + 1) * blocks, :, shard_length - past :], "row", 1)
        for h in range(HALVES)
    ]
    delays = lax.dynamic_index_in_dim(
        beam_delays.reshape(channel_number, n_row, beam_count, A), row_id, 1, keepdims=False
    ).reshape(channel_number * beam_count, A)
    sizes = [size * unit for size in CHUNKS]
    firsts = [sum(sizes[:i]) for i in range(len(sizes))]
    calls = []
    for i, (at, size) in enumerate(zip(firsts, sizes)):
        parts = 2 if size >= LONG * unit else 1
        calls += [(i, at + d * (size // 2), size // parts) for d in range(parts)]
    starts = chan_id * channel_total + jnp.array([at for _, at, _ in calls], jnp.int32)
    base_re, base_im = phasor(delays[None], starts[:, None, None], 1.0 / math.sqrt(A))
    step_re, step_im = phasor(delays, 1, 1.0)
    back = synth_table()
    spread = spread_table(antenna_flags, chan_id, channel_number, block_list)

    taps, table = tap_table(), dft_rows(channel_number)
    arrived = []
    for h in range(HALVES):
        if h == HALVES - 1:
            ahead = [p for m in range(1, channel_number) for p, _ in arrived[0][m]]
            before[h], spread, owners, base_re, base_im, step_re, step_im, back, *ahead = (
                lax.optimization_barrier(
                    (before[h], spread, owners, base_re, base_im, step_re, step_im, back, *ahead)
                )
            )
            arrived[0][1:] = [[(p, 0)] for p in ahead]
        parcels = [channel_total]
        if h == HALVES - 1:
            parcels = sizes[:2] + [channel_total - sum(sizes[:2])]
        sent = front(
            samples.reshape(antennas, -1),
            before[h].reshape(antennas // HALVES, -1),
            history.reshape(antennas, -1),
            place,
            taps,
            table,
            h,
            parcels,
        )
        arrived.append([])
        for m in range(channel_number):
            route = [(i, (i + m) % channel_number) for i in range(channel_number)]
            start = 0
            arrived[h].append([])
            for p, size in enumerate(parcels):
                piece = sent[m * len(parcels) + p]
                arrived[h][m].append((lax.ppermute(piece, "chan", route) if m else piece, start))
                start += size
    def chunk_of(i, halves):
        at = firsts[i]
        pieces = []
        for m in range(channel_number):
            for h in halves:
                piece, start = [(p, s) for p, s in arrived[h][m] if s <= at][-1]
                pieces.append((piece, (at - start) * rows_of))
        table = spread if len(halves) > 1 else spread_of_half[halves[0]]
        chunk = into_order(pieces, len(halves), table, unit * rows_of, CHUNKS[i])
        return chunk.reshape(CHUNKS[i] * unit, rows_of, -1)

    whole_steps = (n_row - 1) // 2
    steps = n_row // 2
    everyone = tuple(range(HALVES))
    lanes = [[(i, everyone) for i in range(lane, len(CHUNKS), 2)] for lane in range(2)]
    order = []
    for pair in zip(*lanes):
        for step in range(steps):
            order += [(chunk, step) for chunk in pair]
    passed = {}
    for chunk, _ in order:
        if chunk not in passed:
            start = chunk_of(*chunk)
            passed[chunk] = [[start], [start]]

    def slots_of(i, first, count):
        shift, half = first - firsts[i], sizes[i] // 2
        onwards, backwards = passed[i, everyone]
        held = [[(p, shift, count)] for p in onwards[: whole_steps + 1]]
        if steps > whole_steps:
            far = [(w[-1], 0, half) for w in (onwards, backwards)]
            held.append(far if count > half else far[shift // half :][:1])
        return held + [[(p, shift, count)] for p in backwards[whole_steps:0:-1]]

    visibilities = None
    beams = {}
    waiting = []

    def products(j, seen=True, formed=True):
        nonlocal visibilities
        made = products_of(
            slots_of(*calls[j]),
            place,
            visibilities,
            (base_re[j], base_im[j], step_re, step_im),
            *calls[j][1:],
            channel_total,
            row_count,
            frames,
            seen,
            formed,
        )
        if seen:
            visibilities = made[0]
        if formed:
            beams[j] = made[-1]
        return made

    def to_owners(group):
        value = jnp.concatenate([beams[j] for j in group], axis=0)
        value = value.reshape(-1, channel_number, beam_count, 2 * frames).transpose(1, 2, 0, 3)
        return lax.all_to_all(value, "chan", split_axis=0, concat_axis=0, tiled=True)

    groups = [
        [j for j, (i, _, _) in enumerate(calls) if low <= i < high]
        for low, high in ((0, 4), (4, len(CHUNKS)))
    ]
    arrived_beams = {}

    sent = {}
    for n, (chunk, step) in enumerate(order):
        lane = chunk[0] % 2
        going = [way[-1] for way in passed[chunk]]
        extra = list(sent.get(lane, []))
        if n == 2:
            extra += [arrived[-1][m][-1][0] for m in range(1, channel_number)]
        while waiting and waiting[0][0] <= n:
            j = waiting.pop(0)[1]
            held = lax.optimization_barrier((*going, *products(j), *extra))
            visibilities, beams[j] = held[2:4]
            for g, group in enumerate(groups):
                if j == group[-1]:
                    arrived_beams[g] = to_owners(group)
            going, extra = held[:2], []
        if extra:
            going = lax.optimization_barrier((*going, *extra))[:2]
        if step >= whole_steps:
            half = sizes[chunk[0]] // 2
            going = [going[0][:half], going[1][half:]]
        got = [lax.ppermute(p, "row", r) for p, r in zip(going, (onward, backward))]
        for d in range(2):
            passed[chunk][d].append(got[d])
        sent[lane] = got
        if step == steps - 1 and lane == 1:
            i = chunk[0]
            work = [j for j, call in enumerate(calls) if call[0] in (i - 1, i)]
            for k, j in enumerate(work):
                waiting.append((n + 1 + k * 2 * steps // len(work), j))

    left = [j for _, j in waiting]
    for j in left:
        products(j, seen=False)
    held = lax.optimization_barrier((visibilities, *[beams[j] for j in left]))
    visibilities = held[0]
    for j, value in zip(left, held[1:]):
        beams[j] = value
    for g, group in enumerate(groups):
        if g not in arrived_beams:
            arrived_beams[g] = to_owners(group)
    for j in left:
        products(j, formed=False)
    spectra = jnp.concatenate([arrived_beams[g] for g in range(len(groups))], axis=2)
    spectra = spectra.transpose(1, 0, 2, 3).reshape(beam_count, NCH, 2 * frames)
    beam_series = synthesis(spectra, back, owners, frames)
    return (visibilities, beam_series)


def solution(mesh):
    in_specs = (P(None, "chan", "row"), P(None, "chan", None), P(), P())
    out_specs = (P("chan", None, "row", None), P(("chan", "row"), None, None))
    return jax.shard_map(body, mesh=mesh, in_specs=in_specs, out_specs=out_specs, check_vma=False)
```

```python
import functools
import math

import jax
import jax.numpy as jnp
from jax import lax
from jax.experimental import pallas as pl
from jax.experimental.pallas import tpu as pltpu
from jax.sharding import PartitionSpec as P

A = 1024
FOURIER_LENGTH = 1024
NCH = 512
FILTER_TAPS = 8
BEAMS = 256
LANES = 128
UNITS = 32
CHUNKS = (4, 6, 6, 6, 4, 2, 2, 2)
LONG = 6
EARLY = 3
BLOCK = 4
HALVES = 2
VMEM = pl.BlockSpec(memory_space=pltpu.VMEM)
HBM = pl.BlockSpec(memory_space=pltpu.HBM)


def params(mib):
    return pltpu.CompilerParams(vmem_limit_bytes=mib * 2**20)


def cost(flops, bytes_accessed):
    return pl.CostEstimate(flops=int(3 * flops), bytes_accessed=int(3 * bytes_accessed), transcendentals=0)


def from_behind(block, axis, distance):
    devices = range(lax.axis_size(axis))
    route = [(i - distance, i) for i in devices if i - distance in devices]
    return lax.ppermute(block, axis, route)


def tap_table():
    position = jnp.arange(FILTER_TAPS * FOURIER_LENGTH, dtype=jnp.int32).astype(jnp.float32) + 0.5
    centred = position / FOURIER_LENGTH - FILTER_TAPS / 2.0
    window = 0.5 - 0.5 * jnp.cos(2.0 * math.pi * position / (FILTER_TAPS * FOURIER_LENGTH))
    return (jnp.sinc(centred) * window).reshape(FILTER_TAPS, FOURIER_LENGTH)


def dft_rows(channel_number):
    chan_ids = jnp.arange(NCH, dtype=jnp.int32).reshape(channel_number, 1, -1, 1)
    sample_ids = jnp.arange(FOURIER_LENGTH, dtype=jnp.int32)
    phase_angle = (chan_ids * sample_ids % FOURIER_LENGTH).astype(jnp.float32) * (
        2.0 * math.pi / FOURIER_LENGTH
    )
    scale = 1.0 / math.sqrt(FOURIER_LENGTH)
    table = jnp.concatenate([jnp.cos(phase_angle) * scale, -jnp.sin(phase_angle) * scale], axis=1)
    return table.astype(jnp.bfloat16).reshape(channel_number, -1, FOURIER_LENGTH)


def synth_table():
    chan_ids = jnp.arange(NCH, dtype=jnp.int32)
    sample_ids = jnp.arange(FOURIER_LENGTH, dtype=jnp.int32)
    phase_angle = (chan_ids[:, None] * sample_ids[None, :] % FOURIER_LENGTH).astype(jnp.float32) * (
        2.0 * math.pi / FOURIER_LENGTH
    )
    scale = 1.0 / math.sqrt(NCH)
    return jnp.stack([jnp.cos(phase_angle) * scale, -jnp.sin(phase_angle) * scale], axis=0).astype(
        jnp.bfloat16
    )


def phasor(delays, chan_ids, scale):
    angle = (delays * chan_ids % FOURIER_LENGTH).astype(jnp.float32) * (
        2.0 * math.pi / FOURIER_LENGTH
    )
    return jnp.cos(angle) * scale, -jnp.sin(angle) * scale


def front_kernel(rows, steps, fold, parcels, place, samples, before, history, taps, table, *refs):
    outs, (filtered, wide) = refs[:-2], refs[-2:]
    step = pl.program_id(0)
    frames = samples.shape[1] // FOURIER_LENGTH
    past = FILTER_TAPS - 1
    group = min(16, rows)
    antennas = filtered.shape[1] // fold

    @pl.when(step < steps)
    def _():
        first = place[1] == 0

        def columns(i, carry):
            at = pl.multiple_of(i * LANES, LANES)
            weights = [
                jnp.broadcast_to(taps[t : t + 1, pl.ds(at, LANES)], (group, LANES))
                for t in range(FILTER_TAPS)
            ]
            for g in range(rows // group):
                here = slice(g * group, (g + 1) * group)
                values = []
                for frame in range(past):
                    lanes = pl.ds(at + frame * FOURIER_LENGTH, LANES)
                    values.append(
                        jnp.where(
                            first,
                            history[here, lanes].astype(jnp.float32),
                            before[here, lanes].astype(jnp.float32),
                        )
                    )
                for frame in range(frames):
                    lanes = pl.ds(at + frame * FOURIER_LENGTH, LANES)
                    values.append(samples[here, lanes].astype(jnp.float32))
                for frame in range(frames):
                    total = values[frame] * weights[0]
                    for t in range(1, FILTER_TAPS):
                        total = total + values[frame + t] * weights[t]
                    to = (frame % fold) * antennas + g * group
                    filtered[frame // fold, pl.ds(step * rows + to, group), pl.ds(at, LANES)] = (
                        total.astype(jnp.bfloat16)
                    )
            return carry

        lax.fori_loop(0, FOURIER_LENGTH // LANES, columns, 0)

    count = table.shape[0] // 2
    for m in range(len(outs) // len(parcels)):

        @pl.when(step == steps + m)
        def _(m=m):
            for several in range(frames // fold):
                got = lax.dot_general(
                    table[...],
                    filtered[several],
                    (((1,), (1,)), ((), ())),
                    preferred_element_type=jnp.float32,
                )
                for part in range(fold):
                    frame = several * fold + part
                    lanes = slice(part * antennas, (part + 1) * antennas)
                    wide[pl.ds(frame, count, stride=2 * frames), :] = got[:count, lanes]
                    wide[pl.ds(frames + frame, count, stride=2 * frames), :] = got[count:, lanes]
            start = 0
            for p, size in enumerate(parcels):
                outs[m * len(parcels) + p][...] = wide[
                    start * 2 * frames : (start + size) * 2 * frames, :
                ].astype(jnp.bfloat16)
                start += size


def front(samples, before, history, place, taps, table, half, parcels):
    antennas = before.shape[0]
    length = samples.shape[1]
    frames = length // FOURIER_LENGTH
    channel_number, channel_total = table.shape[0], table.shape[1] // 2
    rows = min(32, antennas)
    steps = antennas // rows
    fold = math.gcd(frames, max(1, 256 // antennas))
    past = (FILTER_TAPS - 1) * FOURIER_LENGTH
    grid_spec = pltpu.PrefetchScalarGridSpec(
        num_scalar_prefetch=1,
        grid=(steps + channel_number,),
        in_specs=[
            pl.BlockSpec(
                (rows, length), lambda i, s: (half * steps + jnp.minimum(i, steps - 1), 0)
            ),
            pl.BlockSpec((rows, past), lambda i, s: (jnp.minimum(i, steps - 1), 0)),
            pl.BlockSpec(
                (rows, past), lambda i, s: (half * steps + jnp.minimum(i, steps - 1), 0)
            ),
            VMEM,
            pl.BlockSpec(
                (None, 2 * channel_total, FOURIER_LENGTH),
                lambda i, s: (lax.rem(s[0] + jnp.maximum(i - steps, 0), channel_number), 0, 0),
            ),
        ],
        out_specs=[VMEM] * (channel_number * len(parcels)),
        scratch_shapes=[
            pltpu.VMEM((frames // fold, fold * antennas, FOURIER_LENGTH), jnp.bfloat16),
            pltpu.VMEM((channel_total * 2 * frames, antennas), jnp.float32),
        ],
    )
    return pl.pallas_call(
        functools.partial(front_kernel, rows, steps, fold, parcels),
        grid_spec=grid_spec,
        out_shape=[
            jax.ShapeDtypeStruct((size * 2 * frames, antennas), jnp.bfloat16)
            for _ in range(channel_number)
            for size in parcels
        ],
        compiler_params=params(16),
        cost_estimate=cost(2 * antennas * frames * FOURIER_LENGTH * 2 * NCH * 2, 8 * 2**20),
        name="front",
    )(place, samples, before, history, taps, table)


def order_kernel(number, halves, *refs):
    pieces, spread, out = refs[:-2], refs[-2], refs[-1]
    total = None
    for m in range(number):
        left = jnp.concatenate(
            [piece[...] for piece in pieces[m * halves : (m + 1) * halves]], axis=1
        )
        got = jnp.dot(left, spread[m], preferred_element_type=jnp.float32)
        total = got if total is None else total + got
    out[...] = total.astype(jnp.bfloat16)


def into_order(pieces, halves, spread, block, blocks):
    number = len(pieces) // halves
    rows = block * blocks
    width = spread.shape[2]
    return pl.pallas_call(
        functools.partial(order_kernel, number, halves),
        grid=(blocks,),
        in_specs=[
            pl.BlockSpec((block, p.shape[1]), lambda i, at=at: (at // block + i, 0))
            for p, at in pieces
        ]
        + [VMEM],
        out_specs=pl.BlockSpec((block, width), lambda i: (i, 0)),
        out_shape=jax.ShapeDtypeStruct((rows, width), jnp.bfloat16),
        compiler_params=params(10),
        cost_estimate=cost(2 * rows * width * width, rows * width * 4),
        name="into_order",
    )(*[p for p, _ in pieces], spread)


def spread_table(antenna_flags, chan_id, channel_number, block_list):
    per_shard = A // (channel_number * block_list)
    block = (chan_id - jnp.arange(channel_number, dtype=jnp.int32)) % channel_number
    own = jnp.arange(block_list * per_shard, dtype=jnp.int32)
    target = (
        (own // per_shard) * (A // block_list) + block[:, None] * per_shard + own % per_shard
    )
    hit = target[:, :, None] == jnp.arange(A, dtype=jnp.int32)
    return jnp.where(hit, antenna_flags, 0).astype(jnp.bfloat16)


def products_kernel(ends, frames, aliased, seen, formed, place, *refs):
    number = len(ends)
    count = sum(map(len, ends))
    pieces = iter(refs[:count])
    sources = [[next(pieces) for _ in slot] for slot in ends]
    base_re, base_im, step_re, step_im = refs[count : count + 4] if formed else [None] * 4
    outs = refs[count + 4 * formed + aliased :]
    out = outs[0] if seen else None
    beam_out, state_re, state_im = outs[seen:] if formed else [None] * 3
    block, rows = sources[0][0].shape[:2]
    half = rows // 2
    step = pl.program_id(0)

    if formed:

        @pl.when(step == 0)
        def _():
            state_re[...] = base_re[...]
            state_im[...] = base_im[...]

    def slots(i, lanes):
        found = []
        for slot, end in zip(sources, ends):
            value = slot[-1][i, :, lanes]
            for source, last in zip(slot[-2::-1], end[-2::-1]):
                value = jnp.where(step < last, source[i, :, lanes], value)
            found.append(value)
        return jnp.concatenate(found, axis=0)

    def visibilities(i, everything):
        row_count = out.shape[2]
        own_lanes = pl.ds(pl.multiple_of(place[1] * row_count, row_count), row_count)
        wide = slots(i, own_lanes).astype(jnp.float32)
        swapped = jnp.concatenate(
            [
                part
                for s in range(number)
                for part in (
                    wide[(2 * s + 1) * half : (2 * s + 2) * half],
                    -wide[2 * s * half : (2 * s + 1) * half],
                )
            ],
            axis=0,
        )
        left = jnp.concatenate([wide.T, swapped.T], axis=0).astype(jnp.bfloat16)
        got = jnp.dot(left, everything, preferred_element_type=jnp.float32)
        got = (got * (1.0 / frames)).astype(jnp.bfloat16)
        out[i, 0] = got[:row_count]
        out[i, 1] = got[row_count:]

    def beams(i, everything):
        now_re, now_im = state_re[...], state_im[...]
        weights = jnp.concatenate([now_re, now_im], axis=0).astype(jnp.bfloat16)
        state_re[...] = now_re * step_re[...] - now_im * step_im[...]
        state_im[...] = now_re * step_im[...] + now_im * step_re[...]
        got = lax.dot_general(
            weights, everything, (((1,), (1,)), ((), ())), preferred_element_type=jnp.float32
        )
        direct, crossed = jnp.split(got, 2, axis=0)
        width = got.shape[1]
        lane = lax.broadcasted_iota(jnp.int32, crossed.shape, 1)
        real_lane = lax.rem(lane, 2 * half) < half
        crossed = jnp.where(
            real_lane,
            -pltpu.roll(crossed, width - half, 1),
            pltpu.roll(crossed, half, 1),
        )
        beam_out[i] = (direct + crossed).astype(jnp.bfloat16)

    for i in range(block):
        everything = slots(i, slice(None))
        if seen:
            visibilities(i, everything)
        if formed:
            beams(i, everything)


def products_of(
    pieces, place, target, weights, first, count, channel_total, row_count, frames, seen, formed
):
    number = len(pieces)
    rows = pieces[0][0][0].shape[1]
    beams = weights[0].shape[0]
    block = math.gcd(first, BLOCK, *[n for slot in pieces for _, _, n in slot])
    ends = [[sum(n for _, _, n in slot[: c + 1]) // block for c in range(len(slot))] for slot in pieces]
    in_specs = []
    for slot, end in zip(pieces, ends):
        for (_, at, n), last in zip(slot, end):
            begin = last - n // block
            in_specs.append(
                pl.BlockSpec(
                    (block, rows, A),
                    lambda i, s, at=at // block, begin=begin, last=last: (
                        at + jnp.clip(i, begin, last - 1) - begin,
                        0,
                        0,
                    ),
                )
            )
    pieces = [p for slot in pieces for p, _, _ in slot]
    offset = first // block
    aliased = seen and target is not None
    room = 10 if seen and formed else 56
    out_specs, out_shape = [], []
    if seen:
        out_specs.append(
            pl.BlockSpec((block, 2, row_count, A), lambda i, s: (i + offset, 0, 0, 0))
        )
        out_shape.append(
            jax.ShapeDtypeStruct((channel_total, 2, row_count, A), jnp.bfloat16)
        )
    if formed:
        out_specs.append(pl.BlockSpec((block, beams, number * rows), lambda i, s: (i, 0, 0)))
        out_shape.append(jax.ShapeDtypeStruct((count, beams, number * rows), jnp.bfloat16))
    others = [*weights] * formed + [target] * aliased
    return pl.pallas_call(
        functools.partial(products_kernel, ends, frames, aliased, seen, formed),
        grid_spec=pltpu.PrefetchScalarGridSpec(
            num_scalar_prefetch=1,
            grid=(count // block,),
            in_specs=in_specs
            + [pl.BlockSpec((beams, A), lambda i, s: (0, 0))] * (4 * formed)
            + [HBM] * aliased,
            out_specs=out_specs,
            scratch_shapes=[pltpu.VMEM((beams, A), jnp.float32)] * (2 * formed),
        ),
        out_shape=out_shape,
        input_output_aliases={1 + len(pieces) + 4 * formed: 0} if aliased else {},
        compiler_params=params(room),
        cost_estimate=cost(12 * count * row_count * A * 256, count * row_count * A * 6),
        name="products",
    )(place, *pieces, *others)


def synthesis_kernel(number, half, groups, owners, *refs):
    spectra, tables, out = refs[:groups], refs[groups : 2 * groups], refs[-1]
    beams, wide = out.shape[0], out.shape[2]
    got = None
    for part, table in zip(spectra, tables):
        value = jnp.concatenate(
            [
                jnp.concatenate([part[c, i] for i in range(beams)], axis=1)
                for c in range(part.shape[0])
            ],
            axis=0,
        )
        turned = value.T
        both = [
            jnp.dot(turned, table[e], preferred_element_type=jnp.float32) for e in range(2)
        ]
        got = both if got is None else [a + b for a, b in zip(got, both)]
    for i in range(beams):
        for s in range(number):
            real = (i * number + s) * 2 * half
            rows = pl.ds(pl.multiple_of(owners[s] * half, half), half)
            out[i, rows, :] = got[0][real : real + half] + got[1][real + half : real + 2 * half]


def synthesis(spectra, tables, owners, frames):
    beam_count = spectra[0].shape[1]
    number = owners.shape[0]
    wide = 256
    return pl.pallas_call(
        functools.partial(synthesis_kernel, number, frames // number, len(spectra)),
        grid_spec=pltpu.PrefetchScalarGridSpec(
            num_scalar_prefetch=1,
            grid=(FOURIER_LENGTH // wide,),
            in_specs=[VMEM] * len(spectra)
            + [pl.BlockSpec(t.shape[:2] + (wide,), lambda i, s: (0, 0, i)) for t in tables],
            out_specs=pl.BlockSpec((beam_count, frames, wide), lambda i, s: (0, 0, i)),
        ),
        out_shape=jax.ShapeDtypeStruct((beam_count, frames, FOURIER_LENGTH), jnp.float32),
        compiler_params=params(20),
        cost_estimate=cost(4 * beam_count * NCH * 2 * frames * FOURIER_LENGTH, 8 * 2**20),
        name="synthesis",
    )(owners, *spectra, *tables)


def body(samples, history, antenna_flags, beam_delays):
    channel_number = lax.axis_size("chan")
    n_row = lax.axis_size("row")
    chan_id = lax.axis_index("chan")
    row_id = lax.axis_index("row")
    block_list, antennas_per_shard, shard_length = samples.shape
    frames_per_shard = shard_length // FOURIER_LENGTH
    frames = frames_per_shard * n_row
    channel_total = NCH // channel_number
    row_count = A // n_row
    beam_count = BEAMS // (channel_number * n_row)
    antennas = block_list * antennas_per_shard
    unit = channel_total // UNITS
    rows_of = 2 * frames_per_shard
    place = jnp.stack([chan_id, row_id]).astype(jnp.int32)

    cycle = [i for i in range(n_row) if i % 2 == 0] + [i for i in reversed(range(n_row)) if i % 2]
    onward = [(cycle[i], cycle[(i + 1) % n_row]) for i in range(n_row)]
    backward = [(b, a) for a, b in onward]
    position = jnp.array([cycle.index(i) for i in range(n_row)], jnp.int32)[row_id]
    owners = jnp.array(cycle, jnp.int32)[
        (position - jnp.arange(n_row, dtype=jnp.int32)) % n_row
    ]

    past = (FILTER_TAPS - 1) * FOURIER_LENGTH
    blocks = block_list // HALVES
    taps, table = tap_table(), dft_rows(channel_number)
    tail = samples[:blocks, :, shard_length - past :]
    before = [from_behind(tail, "row", 1)]
    later, table = lax.optimization_barrier((samples, table))
    before.append(from_behind(later[blocks:, :, shard_length - past :], "row", 1))
    delays = lax.dynamic_index_in_dim(
        beam_delays.reshape(channel_number, n_row, beam_count, A), row_id, 1, keepdims=False
    ).reshape(channel_number * beam_count, A)
    sizes = [size * unit for size in CHUNKS]
    firsts = [sum(sizes[:i]) for i in range(len(sizes))]
    calls = []
    for i, (at, size) in enumerate(zip(firsts, sizes)):
        parts = 2 if size >= LONG * unit else 1
        calls += [((i,), at + d * (size // 2), size // parts) for d in range(parts)]
    calls[-2:] = [(calls[-2][0] + calls[-1][0], calls[-2][1], calls[-2][2] + calls[-1][2])]
    starts = chan_id * channel_total + jnp.array([at for _, at, _ in calls], jnp.int32)
    base_re, base_im = phasor(delays[None], starts[:, None, None], 1.0 / math.sqrt(A))
    step_re, step_im = phasor(delays, 1, 1.0)
    cuts = (0, firsts[EARLY], channel_total)
    back = synth_table().reshape(2, channel_number, channel_total, FOURIER_LENGTH)
    back = [
        back[:, :, low:high].reshape(2, -1, FOURIER_LENGTH)
        for low, high in zip(cuts[:-1], cuts[1:])
    ]
    spread = spread_table(antenna_flags, chan_id, channel_number, block_list)

    arrived = []
    for h in range(HALVES):
        if h == HALVES - 1:
            ahead = [p for m in range(1, channel_number) for p, _ in arrived[0][m]]
            before[h], spread, owners, base_re, base_im, step_re, step_im, *held = (
                lax.optimization_barrier(
                    (before[h], spread, owners, base_re, base_im, step_re, step_im, *back, *ahead)
                )
            )
            back, ahead = held[: len(back)], held[len(back) :]
            arrived[0][1:] = [[(p, 0)] for p in ahead]
        parcels = [channel_total]
        if h == HALVES - 1:
            parcels = sizes[:2] + [channel_total - sum(sizes[:2])]
        sent = front(
            samples.reshape(antennas, -1),
            before[h].reshape(antennas // HALVES, -1),
            history.reshape(antennas, -1),
            place,
            taps,
            table,
            h,
            parcels,
        )
        arrived.append([])
        for m in range(channel_number):
            route = [(i, (i + m) % channel_number) for i in range(channel_number)]
            start = 0
            arrived[h].append([])
            for p, size in enumerate(parcels):
                piece = sent[m * len(parcels) + p]
                arrived[h][m].append((lax.ppermute(piece, "chan", route) if m else piece, start))
                start += size
    def chunk_of(i, halves):
        at = firsts[i]
        pieces = []
        for m in range(channel_number):
            for h in halves:
                piece, start = [(p, s) for p, s in arrived[h][m] if s <= at][-1]
                pieces.append((piece, (at - start) * rows_of))
        table = spread if len(halves) > 1 else spread_of_half[halves[0]]
        chunk = into_order(pieces, len(halves), table, unit * rows_of, CHUNKS[i])
        return chunk.reshape(CHUNKS[i] * unit, rows_of, -1)

    whole_steps = (n_row - 1) // 2
    steps = n_row // 2
    everyone = tuple(range(HALVES))
    lanes = [[(i, everyone) for i in range(lane, len(CHUNKS), 2)] for lane in range(2)]
    order = []
    for pair in zip(*lanes):
        for step in range(steps):
            order += [(chunk, step) for chunk in pair]
    passed = {}
    for chunk, _ in order:
        if chunk not in passed:
            start = chunk_of(*chunk)
            passed[chunk] = [[start], [start]]

    def slots_of(chunks, first, count):
        found = []
        for i in chunks:
            shift, half = max(first - firsts[i], 0), sizes[i] // 2
            size = min(count, sizes[i])
            onwards, backwards = passed[i, everyone]
            held = [[(p, shift, size)] for p in onwards[: whole_steps + 1]]
            if steps > whole_steps:
                far = [(w[-1], 0, half) for w in (onwards, backwards)]
                held.append(far if size > half else far[shift // half :][:1])
            held += [[(p, shift, size)] for p in backwards[whole_steps:0:-1]]
            found = [a + b for a, b in zip(found, held)] if found else held
        return found

    visibilities = None
    beams = {}
    waiting = []

    def products(j, seen=True, formed=True):
        nonlocal visibilities
        made = products_of(
            slots_of(*calls[j]),
            place,
            visibilities,
            (base_re[j], base_im[j], step_re, step_im),
            *calls[j][1:],
            channel_total,
            row_count,
            frames,
            seen,
            formed,
        )
        if seen:
            visibilities = made[0]
        if formed:
            beams[j] = made[-1]
        return made

    def to_owners(group):
        value = jnp.concatenate([beams[j] for j in group], axis=0)
        value = value.reshape(-1, channel_number, beam_count, 2 * frames).transpose(1, 2, 0, 3)
        return lax.all_to_all(value, "chan", split_axis=0, concat_axis=0, tiled=True)

    groups = [
        [j for j, (i, _, _) in enumerate(calls) if low <= i[0] < high]
        for low, high in ((0, EARLY), (EARLY, len(CHUNKS)))
    ]
    arrived_beams = {}

    sent = {}
    for n, (chunk, step) in enumerate(order):
        lane = chunk[0] % 2
        going = [way[-1] for way in passed[chunk]]
        extra = list(sent.get(lane, []))
        if n == 2:
            extra += [arrived[-1][m][-1][0] for m in range(1, channel_number)]
        while waiting and waiting[0][0] <= n:
            j = waiting.pop(0)[1]
            held = lax.optimization_barrier((*going, *products(j), *extra))
            visibilities, beams[j] = held[2:4]
            for g, group in enumerate(groups):
                if j == group[-1]:
                    arrived_beams[g] = to_owners(group)
            going, extra = held[:2], []
        if n == len(order) - 1:
            extra.append(arrived_beams[0])
        if extra:
            going = lax.optimization_barrier((*going, *extra))[:2]
        if step >= whole_steps:
            half = sizes[chunk[0]] // 2
            going = [going[0][:half], going[1][half:]]
        got = [lax.ppermute(p, "row", r) for p, r in zip(going, (onward, backward))]
        for d in range(2):
            passed[chunk][d].append(got[d])
        sent[lane] = got
        if step == steps - 1 and lane == 1:
            i = chunk[0]
            work = [j for j, call in enumerate(calls) if call[0][-1] in (i - 1, i)]
            for k, j in enumerate(work):
                waiting.append((n + 1 + k * 2 * steps // len(work), j))

    left = [j for _, j in waiting]
    for j in left:
        products(j, seen=False)
    held = lax.optimization_barrier((visibilities, *[beams[j] for j in left]))
    visibilities = held[0]
    for j, value in zip(left, held[1:]):
        beams[j] = value
    for g, group in enumerate(groups):
        if g not in arrived_beams:
            arrived_beams[g] = to_owners(group)
    for j in left:
        products(j, formed=False)
    beam_series = synthesis(
        [arrived_beams[g] for g in range(len(groups))], back, owners, frames
    )
    return (visibilities, beam_series)


def solution(mesh):
    in_specs = (P(None, "chan", "row"), P(None, "chan", None), P(), P())
    out_specs = (P("chan", None, "row", None), P(("chan", "row"), None, None))
    return jax.shard_map(body, mesh=mesh, in_specs=in_specs, out_specs=out_specs, check_vma=False)
```

```python
import functools
import math

import jax
import jax.numpy as jnp
from jax import lax
from jax.experimental import pallas as pl
from jax.experimental.pallas import tpu as pltpu
from jax.sharding import PartitionSpec as P

A = 1024
FOURIER_LENGTH = 1024
NCH = 512
FILTER_TAPS = 8
BEAMS = 256
LANES = 128
UNITS = 32
CHUNKS = (4, 6, 6, 6, 4, 2, 2, 2)
LONG = 6
EARLY = 3
BLOCK = 4
HALVES = 2
VMEM = pl.BlockSpec(memory_space=pltpu.VMEM)
HBM = pl.BlockSpec(memory_space=pltpu.HBM)


def params(mib):
    return pltpu.CompilerParams(vmem_limit_bytes=mib * 2**20)


def cost(flops, bytes_accessed):
    return pl.CostEstimate(flops=int(3 * flops), bytes_accessed=int(3 * bytes_accessed), transcendentals=0)


def from_behind(block, axis, distance):
    devices = range(lax.axis_size(axis))
    route = [(i - distance, i) for i in devices if i - distance in devices]
    return lax.ppermute(block, axis, route)


def tap_table():
    position = jnp.arange(FILTER_TAPS * FOURIER_LENGTH, dtype=jnp.int32).astype(jnp.float32) + 0.5
    centred = position / FOURIER_LENGTH - FILTER_TAPS / 2.0
    window = 0.5 - 0.5 * jnp.cos(2.0 * math.pi * position / (FILTER_TAPS * FOURIER_LENGTH))
    return (jnp.sinc(centred) * window).reshape(FILTER_TAPS, FOURIER_LENGTH)


def dft_rows(channel_number):
    chan_ids = jnp.arange(NCH, dtype=jnp.int32).reshape(channel_number, 1, -1, 1)
    sample_ids = jnp.arange(FOURIER_LENGTH, dtype=jnp.int32)
    phase_angle = (chan_ids * sample_ids % FOURIER_LENGTH).astype(jnp.float32) * (
        2.0 * math.pi / FOURIER_LENGTH
    )
    scale = 1.0 / math.sqrt(FOURIER_LENGTH)
    table = jnp.concatenate([jnp.cos(phase_angle) * scale, -jnp.sin(phase_angle) * scale], axis=1)
    return table.astype(jnp.bfloat16).reshape(channel_number, -1, FOURIER_LENGTH)


def synth_table():
    chan_ids = jnp.arange(NCH, dtype=jnp.int32)
    sample_ids = jnp.arange(FOURIER_LENGTH, dtype=jnp.int32)
    phase_angle = (chan_ids[:, None] * sample_ids[None, :] % FOURIER_LENGTH).astype(jnp.float32) * (
        2.0 * math.pi / FOURIER_LENGTH
    )
    scale = 1.0 / math.sqrt(NCH)
    return jnp.stack([jnp.cos(phase_angle) * scale, -jnp.sin(phase_angle) * scale], axis=0).astype(
        jnp.bfloat16
    )


def phasor(delays, chan_ids, scale):
    angle = (delays * chan_ids % FOURIER_LENGTH).astype(jnp.float32) * (
        2.0 * math.pi / FOURIER_LENGTH
    )
    return jnp.cos(angle) * scale, -jnp.sin(angle) * scale


def front_kernel(rows, steps, fold, parcels, place, samples, before, history, taps, table, *refs):
    outs, (filtered, wide) = refs[:-2], refs[-2:]
    step = pl.program_id(0)
    frames = samples.shape[1] // FOURIER_LENGTH
    past = FILTER_TAPS - 1
    group = min(16, rows)
    antennas = filtered.shape[1] // fold

    @pl.when(step < steps)
    def _():
        first = place[1] == 0

        def columns(i, carry):
            at = pl.multiple_of(i * LANES, LANES)
            weights = [
                jnp.broadcast_to(taps[t : t + 1, pl.ds(at, LANES)], (group, LANES))
                for t in range(FILTER_TAPS)
            ]
            for g in range(rows // group):
                here = slice(g * group, (g + 1) * group)
                values = []
                for frame in range(past):
                    lanes = pl.ds(at + frame * FOURIER_LENGTH, LANES)
                    values.append(
                        jnp.where(
                            first,
                            history[here, lanes].astype(jnp.float32),
                            before[here, lanes].astype(jnp.float32),
                        )
                    )
                for frame in range(frames):
                    lanes = pl.ds(at + frame * FOURIER_LENGTH, LANES)
                    values.append(samples[here, lanes].astype(jnp.float32))
                for frame in range(frames):
                    total = values[frame] * weights[0]
                    for t in range(1, FILTER_TAPS):
                        total = total + values[frame + t] * weights[t]
                    to = (frame % fold) * antennas + g * group
                    filtered[frame // fold, pl.ds(step * rows + to, group), pl.ds(at, LANES)] = (
                        total.astype(jnp.bfloat16)
                    )
            return carry

        lax.fori_loop(0, FOURIER_LENGTH // LANES, columns, 0)

    count = table.shape[0] // 2
    for m in range(len(outs) // len(parcels)):

        @pl.when(step == steps + m)
        def _(m=m):
            for several in range(frames // fold):
                got = lax.dot_general(
                    table[...],
                    filtered[several],
                    (((1,), (1,)), ((), ())),
                    preferred_element_type=jnp.float32,
                )
                for part in range(fold):
                    frame = several * fold + part
                    lanes = slice(part * antennas, (part + 1) * antennas)
                    wide[pl.ds(frame, count, stride=2 * frames), :] = got[:count, lanes]
                    wide[pl.ds(frames + frame, count, stride=2 * frames), :] = got[count:, lanes]
            start = 0
            for p, size in enumerate(parcels):
                outs[m * len(parcels) + p][...] = wide[
                    start * 2 * frames : (start + size) * 2 * frames, :
                ].astype(jnp.bfloat16)
                start += size


def front(samples, before, history, place, taps, table, half, parcels):
    antennas = before.shape[0]
    length = samples.shape[1]
    frames = length // FOURIER_LENGTH
    channel_number, channel_total = table.shape[0], table.shape[1] // 2
    rows = min(32, antennas)
    steps = antennas // rows
    fold = math.gcd(frames, max(1, 256 // antennas))
    past = (FILTER_TAPS - 1) * FOURIER_LENGTH
    grid_spec = pltpu.PrefetchScalarGridSpec(
        num_scalar_prefetch=1,
        grid=(steps + channel_number,),
        in_specs=[
            pl.BlockSpec(
                (rows, length), lambda i, s: (half * steps + jnp.minimum(i, steps - 1), 0)
            ),
            pl.BlockSpec((rows, past), lambda i, s: (jnp.minimum(i, steps - 1), 0)),
            pl.BlockSpec(
                (rows, past), lambda i, s: (half * steps + jnp.minimum(i, steps - 1), 0)
            ),
            VMEM,
            pl.BlockSpec(
                (None, 2 * channel_total, FOURIER_LENGTH),
                lambda i, s: (lax.rem(s[0] + jnp.maximum(i - steps, 0), channel_number), 0, 0),
            ),
        ],
        out_specs=[VMEM] * (channel_number * len(parcels)),
        scratch_shapes=[
            pltpu.VMEM((frames // fold, fold * antennas, FOURIER_LENGTH), jnp.bfloat16),
            pltpu.VMEM((channel_total * 2 * frames, antennas), jnp.float32),
        ],
    )
    return pl.pallas_call(
        functools.partial(front_kernel, rows, steps, fold, parcels),
        grid_spec=grid_spec,
        out_shape=[
            jax.ShapeDtypeStruct((size * 2 * frames, antennas), jnp.bfloat16)
            for _ in range(channel_number)
            for size in parcels
        ],
        compiler_params=params(16),
        cost_estimate=cost(2 * antennas * frames * FOURIER_LENGTH * 2 * NCH * 2, 8 * 2**20),
        name="front",
    )(place, samples, before, history, taps, table)


def order_kernel(number, halves, *refs):
    pieces, spread, out = refs[:-2], refs[-2], refs[-1]
    total = None
    for m in range(number):
        left = jnp.concatenate(
            [piece[...] for piece in pieces[m * halves : (m + 1) * halves]], axis=1
        )
        got = jnp.dot(left, spread[m], preferred_element_type=jnp.float32)
        total = got if total is None else total + got
    out[...] = total.astype(jnp.bfloat16)


def into_order(pieces, halves, spread, block, blocks):
    number = len(pieces) // halves
    together = math.gcd(blocks, *[at // block for _, at in pieces])
    block, blocks = block * together, blocks // together
    rows = block * blocks
    width = spread.shape[2]
    return pl.pallas_call(
        functools.partial(order_kernel, number, halves),
        grid=(blocks,),
        in_specs=[
            pl.BlockSpec((block, p.shape[1]), lambda i, at=at: (at // block + i, 0))
            for p, at in pieces
        ]
        + [VMEM],
        out_specs=pl.BlockSpec((block, width), lambda i: (i, 0)),
        out_shape=jax.ShapeDtypeStruct((rows, width), jnp.bfloat16),
        compiler_params=params(10),
        cost_estimate=cost(2 * rows * width * width, rows * width * 4),
        name="into_order",
    )(*[p for p, _ in pieces], spread)


def spread_table(antenna_flags, chan_id, channel_number, block_list):
    per_shard = A // (channel_number * block_list)
    block = (chan_id - jnp.arange(channel_number, dtype=jnp.int32)) % channel_number
    own = jnp.arange(block_list * per_shard, dtype=jnp.int32)
    target = (
        (own // per_shard) * (A // block_list) + block[:, None] * per_shard + own % per_shard
    )
    hit = target[:, :, None] == jnp.arange(A, dtype=jnp.int32)
    return jnp.where(hit, antenna_flags, 0).astype(jnp.bfloat16)


def products_kernel(ends, frames, aliased, seen, formed, place, *refs):
    number = len(ends)
    count = sum(map(len, ends))
    pieces = iter(refs[:count])
    sources = [[next(pieces) for _ in slot] for slot in ends]
    base_re, base_im, step_re, step_im = refs[count : count + 4] if formed else [None] * 4
    outs = refs[count + 4 * formed + aliased :]
    out = outs[0] if seen else None
    beam_out, state_re, state_im = outs[seen:] if formed else [None] * 3
    block, rows = sources[0][0].shape[:2]
    half = rows // 2
    step = pl.program_id(0)

    if formed:

        @pl.when(step == 0)
        def _():
            state_re[...] = base_re[...]
            state_im[...] = base_im[...]

    def slots(i, lanes):
        found = []
        for slot, end in zip(sources, ends):
            value = slot[-1][i, :, lanes]
            for source, last in zip(slot[-2::-1], end[-2::-1]):
                value = jnp.where(step < last, source[i, :, lanes], value)
            found.append(value)
        return jnp.concatenate(found, axis=0)

    def visibilities(i, everything):
        row_count = out.shape[2]
        own_lanes = pl.ds(pl.multiple_of(place[1] * row_count, row_count), row_count)
        wide = slots(i, own_lanes).astype(jnp.float32)
        swapped = jnp.concatenate(
            [
                part
                for s in range(number)
                for part in (
                    wide[(2 * s + 1) * half : (2 * s + 2) * half],
                    -wide[2 * s * half : (2 * s + 1) * half],
                )
            ],
            axis=0,
        )
        left = jnp.concatenate([wide.T, swapped.T], axis=0).astype(jnp.bfloat16)
        got = jnp.dot(left, everything, preferred_element_type=jnp.float32)
        got = (got * (1.0 / frames)).astype(jnp.bfloat16)
        out[i, 0] = got[:row_count]
        out[i, 1] = got[row_count:]

    def beams(i, everything):
        now_re, now_im = state_re[...], state_im[...]
        weights = jnp.concatenate([now_re, now_im], axis=0).astype(jnp.bfloat16)
        state_re[...] = now_re * step_re[...] - now_im * step_im[...]
        state_im[...] = now_re * step_im[...] + now_im * step_re[...]
        got = lax.dot_general(
            weights, everything, (((1,), (1,)), ((), ())), preferred_element_type=jnp.float32
        )
        direct, crossed = jnp.split(got, 2, axis=0)
        width = got.shape[1]
        lane = lax.broadcasted_iota(jnp.int32, crossed.shape, 1)
        real_lane = lax.rem(lane, 2 * half) < half
        crossed = jnp.where(
            real_lane,
            -pltpu.roll(crossed, width - half, 1),
            pltpu.roll(crossed, half, 1),
        )
        beam_out[i] = (direct + crossed).astype(jnp.bfloat16)

    for i in range(block):
        everything = slots(i, slice(None))
        if seen:
            visibilities(i, everything)
        if formed:
            beams(i, everything)


def products_of(
    pieces, place, target, weights, first, count, channel_total, row_count, frames, seen, formed
):
    number = len(pieces)
    rows = pieces[0][0][0].shape[1]
    beams = weights[0].shape[0]
    block = math.gcd(first, BLOCK, *[n for slot in pieces for _, _, n in slot])
    ends = [[sum(n for _, _, n in slot[: c + 1]) // block for c in range(len(slot))] for slot in pieces]
    in_specs = []
    for slot, end in zip(pieces, ends):
        for (_, at, n), last in zip(slot, end):
            begin = last - n // block
            in_specs.append(
                pl.BlockSpec(
                    (block, rows, A),
                    lambda i, s, at=at // block, begin=begin, last=last: (
                        at + jnp.clip(i, begin, last - 1) - begin,
                        0,
                        0,
                    ),
                )
            )
    pieces = [p for slot in pieces for p, _, _ in slot]
    offset = first // block
    aliased = seen and target is not None
    room = 10 if seen and formed else 56
    out_specs, out_shape = [], []
    if seen:
        out_specs.append(
            pl.BlockSpec((block, 2, row_count, A), lambda i, s: (i + offset, 0, 0, 0))
        )
        out_shape.append(
            jax.ShapeDtypeStruct((channel_total, 2, row_count, A), jnp.bfloat16)
        )
    if formed:
        out_specs.append(pl.BlockSpec((block, beams, number * rows), lambda i, s: (i, 0, 0)))
        out_shape.append(jax.ShapeDtypeStruct((count, beams, number * rows), jnp.bfloat16))
    others = [*weights] * formed + [target] * aliased
    return pl.pallas_call(
        functools.partial(products_kernel, ends, frames, aliased, seen, formed),
        grid_spec=pltpu.PrefetchScalarGridSpec(
            num_scalar_prefetch=1,
            grid=(count // block,),
            in_specs=in_specs
            + [pl.BlockSpec((beams, A), lambda i, s: (0, 0))] * (4 * formed)
            + [HBM] * aliased,
            out_specs=out_specs,
            scratch_shapes=[pltpu.VMEM((beams, A), jnp.float32)] * (2 * formed),
        ),
        out_shape=out_shape,
        input_output_aliases={1 + len(pieces) + 4 * formed: 0} if aliased else {},
        compiler_params=params(room),
        cost_estimate=cost(12 * count * row_count * A * 256, count * row_count * A * 6),
        name="products",
    )(place, *pieces, *others)


def synthesis_kernel(number, half, groups, owners, *refs):
    spectra, tables, out = refs[:groups], refs[groups : 2 * groups], refs[-1]
    beams, wide = out.shape[0], out.shape[2]
    got = None
    for part, table in zip(spectra, tables):
        value = jnp.concatenate(
            [
                jnp.concatenate([part[c, i] for i in range(beams)], axis=1)
                for c in range(part.shape[0])
            ],
            axis=0,
        )
        turned = value.T
        both = [
            jnp.dot(turned, table[e], preferred_element_type=jnp.float32) for e in range(2)
        ]
        got = both if got is None else [a + b for a, b in zip(got, both)]
    for i in range(beams):
        for s in range(number):
            real = (i * number + s) * 2 * half
            rows = pl.ds(pl.multiple_of(owners[s] * half, half), half)
            out[i, rows, :] = got[0][real : real + half] + got[1][real + half : real + 2 * half]


def synthesis(spectra, tables, owners, frames):
    beam_count = spectra[0].shape[1]
    number = owners.shape[0]
    wide = 256
    return pl.pallas_call(
        functools.partial(synthesis_kernel, number, frames // number, len(spectra)),
        grid_spec=pltpu.PrefetchScalarGridSpec(
            num_scalar_prefetch=1,
            grid=(FOURIER_LENGTH // wide,),
            in_specs=[VMEM] * len(spectra)
            + [pl.BlockSpec(t.shape[:2] + (wide,), lambda i, s: (0, 0, i)) for t in tables],
            out_specs=pl.BlockSpec((beam_count, frames, wide), lambda i, s: (0, 0, i)),
        ),
        out_shape=jax.ShapeDtypeStruct((beam_count, frames, FOURIER_LENGTH), jnp.float32),
        compiler_params=params(20),
        cost_estimate=cost(4 * beam_count * NCH * 2 * frames * FOURIER_LENGTH, 8 * 2**20),
        name="synthesis",
    )(owners, *spectra, *tables)


def body(samples, history, antenna_flags, beam_delays):
    channel_number = lax.axis_size("chan")
    n_row = lax.axis_size("row")
    chan_id = lax.axis_index("chan")
    row_id = lax.axis_index("row")
    block_list, antennas_per_shard, shard_length = samples.shape
    frames_per_shard = shard_length // FOURIER_LENGTH
    frames = frames_per_shard * n_row
    channel_total = NCH // channel_number
    row_count = A // n_row
    beam_count = BEAMS // (channel_number * n_row)
    antennas = block_list * antennas_per_shard
    unit = channel_total // UNITS
    rows_of = 2 * frames_per_shard
    place = jnp.stack([chan_id, row_id]).astype(jnp.int32)

    cycle = [i for i in range(n_row) if i % 2 == 0] + [i for i in reversed(range(n_row)) if i % 2]
    onward = [(cycle[i], cycle[(i + 1) % n_row]) for i in range(n_row)]
    backward = [(b, a) for a, b in onward]
    position = jnp.array([cycle.index(i) for i in range(n_row)], jnp.int32)[row_id]
    owners = jnp.array(cycle, jnp.int32)[
        (position - jnp.arange(n_row, dtype=jnp.int32)) % n_row
    ]

    past = (FILTER_TAPS - 1) * FOURIER_LENGTH
    blocks = block_list // HALVES
    taps, table = tap_table(), dft_rows(channel_number)
    tail = samples[:blocks, :, shard_length - past :]
    before = [from_behind(tail, "row", 1)]
    later, table = lax.optimization_barrier((samples, table))
    before.append(from_behind(later[blocks:, :, shard_length - past :], "row", 1))
    delays = lax.dynamic_index_in_dim(
        beam_delays.reshape(channel_number, n_row, beam_count, A), row_id, 1, keepdims=False
    ).reshape(channel_number * beam_count, A)
    sizes = [size * unit for size in CHUNKS]
    firsts = [sum(sizes[:i]) for i in range(len(sizes))]
    calls = []
    for i, (at, size) in enumerate(zip(firsts, sizes)):
        parts = 2 if size >= LONG * unit else 1
        calls += [((i,), at + d * (size // 2), size // parts) for d in range(parts)]
    calls[-2:] = [(calls[-2][0] + calls[-1][0], calls[-2][1], calls[-2][2] + calls[-1][2])]
    starts = chan_id * channel_total + jnp.array([at for _, at, _ in calls], jnp.int32)
    base_re, base_im = phasor(delays[None], starts[:, None, None], 1.0 / math.sqrt(A))
    step_re, step_im = phasor(delays, 1, 1.0)
    cuts = (0, firsts[EARLY], channel_total)
    back = synth_table().reshape(2, channel_number, channel_total, FOURIER_LENGTH)
    back = [
        back[:, :, low:high].reshape(2, -1, FOURIER_LENGTH)
        for low, high in zip(cuts[:-1], cuts[1:])
    ]
    spread = spread_table(antenna_flags, chan_id, channel_number, block_list)

    arrived = []
    for h in range(HALVES):
        if h == HALVES - 1:
            ahead = [p for m in range(1, channel_number) for p, _ in arrived[0][m]]
            before[h], spread, owners, base_re, base_im, step_re, step_im, *held = (
                lax.optimization_barrier(
                    (before[h], spread, owners, base_re, base_im, step_re, step_im, *back, *ahead)
                )
            )
            back, ahead = held[: len(back)], held[len(back) :]
            arrived[0][1:] = [[(p, 0)] for p in ahead]
        parcels = [channel_total]
        if h == HALVES - 1:
            parcels = sizes[:2] + [channel_total - sum(sizes[:2])]
        sent = front(
            samples.reshape(antennas, -1),
            before[h].reshape(antennas // HALVES, -1),
            history.reshape(antennas, -1),
            place,
            taps,
            table,
            h,
            parcels,
        )
        arrived.append([])
        for m in range(channel_number):
            route = [(i, (i + m) % channel_number) for i in range(channel_number)]
            start = 0
            arrived[h].append([])
            for p, size in enumerate(parcels):
                piece = sent[m * len(parcels) + p]
                arrived[h][m].append((lax.ppermute(piece, "chan", route) if m else piece, start))
                start += size
    def chunk_of(i, halves):
        at = firsts[i]
        pieces = []
        for m in range(channel_number):
            for h in halves:
                piece, start = [(p, s) for p, s in arrived[h][m] if s <= at][-1]
                pieces.append((piece, (at - start) * rows_of))
        table = spread if len(halves) > 1 else spread_of_half[halves[0]]
        chunk = into_order(pieces, len(halves), table, unit * rows_of, CHUNKS[i])
        return chunk.reshape(CHUNKS[i] * unit, rows_of, -1)

    whole_steps = (n_row - 1) // 2
    steps = n_row // 2
    everyone = tuple(range(HALVES))
    lanes = [[(i, everyone) for i in range(lane, len(CHUNKS), 2)] for lane in range(2)]
    order = []
    for pair in zip(*lanes):
        for step in range(steps):
            order += [(chunk, step) for chunk in pair]
    passed = {}
    for chunk, _ in order:
        if chunk not in passed:
            start = chunk_of(*chunk)
            passed[chunk] = [[start], [start]]

    def slots_of(chunks, first, count):
        found = []
        for i in chunks:
            shift, half = max(first - firsts[i], 0), sizes[i] // 2
            size = min(count, sizes[i])
            onwards, backwards = passed[i, everyone]
            held = [[(p, shift, size)] for p in onwards[: whole_steps + 1]]
            if steps > whole_steps:
                far = [(w[-1], 0, half) for w in (onwards, backwards)]
                held.append(far if size > half else far[shift // half :][:1])
            held += [[(p, shift, size)] for p in backwards[whole_steps:0:-1]]
            found = [a + b for a, b in zip(found, held)] if found else held
        return found

    visibilities = None
    beams = {}
    waiting = []

    def products(j, seen=True, formed=True):
        nonlocal visibilities
        made = products_of(
            slots_of(*calls[j]),
            place,
            visibilities,
            (base_re[j], base_im[j], step_re, step_im),
            *calls[j][1:],
            channel_total,
            row_count,
            frames,
            seen,
            formed,
        )
        if seen:
            visibilities = made[0]
        if formed:
            beams[j] = made[-1]
        return made

    def to_owners(group):
        value = jnp.concatenate([beams[j] for j in group], axis=0)
        value = value.reshape(-1, channel_number, beam_count, 2 * frames).transpose(1, 2, 0, 3)
        return lax.all_to_all(value, "chan", split_axis=0, concat_axis=0, tiled=True)

    groups = [
        [j for j, (i, _, _) in enumerate(calls) if low <= i[0] < high]
        for low, high in ((0, EARLY), (EARLY, len(CHUNKS)))
    ]
    arrived_beams = {}

    sent = {}
    for n, (chunk, step) in enumerate(order):
        lane = chunk[0] % 2
        going = [way[-1] for way in passed[chunk]]
        extra = list(sent.get(lane, []))
        if n == 2:
            extra += [arrived[-1][m][-1][0] for m in range(1, channel_number)]
        while waiting and waiting[0][0] <= n:
            j = waiting.pop(0)[1]
            held = lax.optimization_barrier((*going, *products(j), *extra))
            visibilities, beams[j] = held[2:4]
            for g, group in enumerate(groups):
                if j == group[-1]:
                    arrived_beams[g] = to_owners(group)
            going, extra = held[:2], []
        if n == len(order) - 1:
            extra.append(arrived_beams[0])
        if extra:
            going = lax.optimization_barrier((*going, *extra))[:2]
        if step >= whole_steps:
            half = sizes[chunk[0]] // 2
            going = [going[0][:half], going[1][half:]]
        got = [lax.ppermute(p, "row", r) for p, r in zip(going, (onward, backward))]
        for d in range(2):
            passed[chunk][d].append(got[d])
        sent[lane] = got
        if step == steps - 1 and lane == 1:
            i = chunk[0]
            work = [j for j, call in enumerate(calls) if call[0][-1] in (i - 1, i)]
            for k, j in enumerate(work):
                waiting.append((n + 1 + k * 2 * steps // len(work), j))

    left = [j for _, j in waiting]
    for j in left:
        products(j, seen=False)
    held = lax.optimization_barrier((visibilities, *[beams[j] for j in left]))
    visibilities = held[0]
    for j, value in zip(left, held[1:]):
        beams[j] = value
    for g, group in enumerate(groups):
        if g not in arrived_beams:
            arrived_beams[g] = to_owners(group)
    for j in left:
        products(j, formed=False)
    beam_series = synthesis(
        [arrived_beams[g] for g in range(len(groups))], back, owners, frames
    )
    return (visibilities, beam_series)


def solution(mesh):
    in_specs = (P(None, "chan", "row"), P(None, "chan", None), P(), P())
    out_specs = (P("chan", None, "row", None), P(("chan", "row"), None, None))
    return jax.shard_map(body, mesh=mesh, in_specs=in_specs, out_specs=out_specs, check_vma=False)
```
